32 devices in a mesh: group: 4 (over z), replica: 8 (over y, x, core).
Axes of the slice: x: 2, y: 2, z: 4, core: 2. Of those that a mesh axis runs over, the one named last changes fastest.
Arguments:
- hidden_in: bfloat16 [8192, 640], P(('group', 'replica')), may hold values from -63 to 63, as said below
- cotangent: bfloat16 [8192, 640], P(('group', 'replica')), may hold values from -15 to 15, as said below
- segment_ids: int32 [8192], P(('group', 'replica')), may hold values from 0 to 1, as said below
- positions: int32 [8192], P(('group', 'replica')), may hold values from 0 to 16382, as said below
- w_qkv: bfloat16 [640, 1536], P('group'), may hold values from -0.25 to 0.25
- w_out: bfloat16 [1024, 640], P('group'), may hold values from -0.1875 to 0.1875
- w_gate_up: bfloat16 [640, 4096], P('group'), may hold values from -0.25 to 0.25
- w_down: bfloat16 [2048, 640], P('group'), may hold values from -0.125 to 0.125
- norm_gains: float32 [3072], replicated, may hold values from -0.08 to 0.08
- first_qkv: float32 [640, 1536], P('group', 'replica'), may hold values from -128 to 128
- first_out: float32 [1024, 640], P('group', 'replica'), may hold values from -128 to 128
- first_gate_up: float32 [640, 4096], P('group', 'replica'), may hold values from -128 to 128
- first_down: float32 [2048, 640], P('group', 'replica'), may hold values from -128 to 128
- first_gains: float32 [3072], P(('group', 'replica')), may hold values from -128 to 128
- second_qkv: float32 [640, 1536], P('group', 'replica'), may hold values from 16.384 to 262.144
- second_out: float32 [1024, 640], P('group', 'replica'), may hold values from 16.384 to 262.144
- second_gate_up: float32 [640, 4096], P('group', 'replica'), may hold values from 16.384 to 262.144
- second_down: float32 [2048, 640], P('group', 'replica'), may hold values from 16.384 to 262.144
- second_gains: float32 [3072], P(('group', 'replica')), may hold values from 16.384 to 262.144
Outputs:
- block_out: bfloat16 [8192, 640], P(('group', 'replica'))
- grad_in: bfloat16 [8192, 640], P(('group', 'replica'))
- grad_qkv: float32 [640, 1536], P('group', 'replica')
- grad_out: float32 [1024, 640], P('group', 'replica')
- grad_gate_up: float32 [640, 4096], P('group', 'replica')
- grad_down: float32 [2048, 640], P('group', 'replica')
- grad_gains: float32 [3072], P(('group', 'replica'))
- moment_qkv: float32 [640, 1536], P('group', 'replica')
- moment_out: float32 [1024, 640], P('group', 'replica')
- moment_gate_up: float32 [640, 4096], P('group', 'replica')
- moment_down: float32 [2048, 640], P('group', 'replica')
- moment_gains: float32 [3072], P(('group', 'replica'))
- new_qkv: float32 [640, 1536], P('group', 'replica')
- new_out: float32 [1024, 640], P('group', 'replica')
- new_gate_up: float32 [640, 4096], P('group', 'replica')
- new_down: float32 [2048, 640], P('group', 'replica')
- new_gains: float32 [3072], P(('group', 'replica'))
The draws below stay inside these ranges and needn't reach their ends.
Inputs may be any that keep to these rules, and one draw needn't show every extreme that they name: `hidden_in`: entries are real-valued, of both signs, with row and column scales that differ. `cotangent`: entries are real-valued, of both signs. `segment_ids`: sequence numbers never fall along the tokens; every sequence other than the first and the last holds exactly 8192 tokens. Within a sequence the positions rise by one from token to token.
All inputs are finite; a program needn't handle non-finite values.
Results may differ from the reference program's by a relative error of at most 0.018.
Values may be sent and summed in bfloat16 or wider, within the bound.
A program may use at most 128 MiB of HBM per device.

```python
import math
import jax
import jax.numpy as jnp
from jax import lax

D = 640
H = 4
HD = 256
FF = 2048
WINDOW = 512
STEP = 10
TOK_DEV = 256
TOKENS = 8192
SEQ = 8192
GAINS = 3072
N_GROUP = 4
N_REPLICA = 8


def document_layout(key):
    offset_key, start_key = jax.random.split(key)
    offset = jax.random.randint(offset_key, (), 1, SEQ)
    shifted = jnp.arange(TOKENS, dtype=jnp.int32) + offset
    segment = shifted // SEQ
    starts = jax.random.randint(start_key, (TOKENS // SEQ + 1,), 0, SEQ)
    starts = starts.at[0].set(SEQ - 1)
    starts = starts.at[TOKENS // SEQ].set(0)
    position = shifted % SEQ + starts[segment]
    return (segment.astype(jnp.int32), position.astype(jnp.int32))


def draw_segment_ids(key, part):
    segment, position = document_layout(key)
    return segment


def draw_positions(key, part):
    segment, position = document_layout(key)
    return position


def draw_hidden_in(key, part):
    key = jax.random.fold_in(key, 7)
    keys = jax.random.split(key, 3)
    base = jnp.clip(jax.random.normal(keys[0], (TOKENS, D), jnp.float32), -5.0, 5.0)
    spread = math.log(10.0)
    rows = jnp.exp(jax.random.uniform(keys[1], (TOKENS, 1), jnp.float32, 0.0, spread))
    columns = jnp.exp(jax.random.uniform(keys[2], (1, D), jnp.float32, 0.0, spread))
    return (base * rows * columns / 8.0).astype(jnp.bfloat16)


def draw_cotangent(key, part):
    key = jax.random.fold_in(key, 11)
    shard = jnp.arange(TOKENS, dtype=jnp.int32) // TOK_DEV
    along_replica = (shard % N_REPLICA).astype(jnp.float32) / max(N_REPLICA - 1, 1)
    along_group = (shard // N_REPLICA).astype(jnp.float32) / max(N_GROUP - 1, 1)
    base = jnp.clip(jax.random.normal(key, (TOKENS, D), jnp.float32), -5.0, 5.0)
    rise = (1.0 + 2.0 * along_replica) * (1.0 + 2.0 * along_group) / 3.0
    return (base * rise[:, None]).astype(jnp.bfloat16)


def block_levels(rng, shape, cuts, low, largest):
    def one(dim, shards_of):
        heights = jax.random.uniform(jax.random.fold_in(jax.random.fold_in(rng, 6), dim), (shards_of,), jnp.float32, low / len(cuts), largest / len(cuts))
        return jnp.repeat(jnp.exp(heights), shape[dim] // shards_of).reshape((-1,) + (1,) * (len(shape) - dim - 1))

    level = one(*cuts[0])
    for cut in cuts[1:]:
        level = level * one(*cut)
    return level


def normal_values(own_key, extent, deviation, most, pieces=(), kind=jnp.bfloat16):
    factor_of = block_levels(own_key, extent, pieces, -0.22, 0.18) if pieces else 1.0
    array = jax.random.normal(own_key, extent, jnp.float32) * deviation * factor_of
    return jnp.minimum(jnp.maximum(array, -most), most).astype(kind)


def setup_inputs(seed: int = 0) -> dict:
    arg_keys = jax.random.split(jax.random.key(seed), 20)
    return {
        "hidden_in": draw_hidden_in(jax.random.fold_in(arg_keys[19], 71), 0),
        "cotangent": draw_cotangent(jax.random.fold_in(arg_keys[19], 71), 0),
        "segment_ids": draw_segment_ids(jax.random.fold_in(arg_keys[19], 71), 0),
        "positions": draw_positions(jax.random.fold_in(arg_keys[19], 71), 0),
        "w_qkv": normal_values(arg_keys[4], (D, (H + 2) * HD), D ** -0.5, 0.25, ((0, 4),)),
        "w_out": normal_values(arg_keys[5], (H * HD, D), (H * HD) ** -0.5, 0.1875, ((0, 4),)),
        "w_gate_up": normal_values(arg_keys[6], (D, 2 * FF), D ** -0.5, 0.25, ((0, 4),)),
        "w_down": normal_values(arg_keys[7], (FF, D), FF ** -0.5, 0.125, ((0, 4),)),
        "norm_gains": jnp.clip(jax.random.uniform(arg_keys[8], (GAINS,), jnp.float32, -0.08, 0.08), -0.08, 0.08),
        "first_qkv": normal_values(arg_keys[9], (D, (H + 2) * HD), (0.222 * TOKENS ** 0.5), 128.0, ((0, 4), (1, 8)), jnp.float32),
        "first_out": normal_values(arg_keys[10], (H * HD, D), (0.222 * TOKENS ** 0.5), 128.0, ((0, 4), (1, 8)), jnp.float32),
        "first_gate_up": normal_values(arg_keys[11], (D, 2 * FF), (0.222 * TOKENS ** 0.5), 128.0, ((0, 4), (1, 8)), jnp.float32),
        "first_down": normal_values(arg_keys[12], (FF, D), (0.222 * TOKENS ** 0.5), 128.0, ((0, 4), (1, 8)), jnp.float32),
        "first_gains": normal_values(arg_keys[13], (GAINS,), (0.222 * TOKENS ** 0.5), 128.0, ((0, 32),), jnp.float32),
        "second_qkv": jnp.clip(jnp.exp(math.log(262.144) - 2.7725887 * jax.random.uniform(arg_keys[14], (D, (H + 2) * HD), jnp.float32) ** block_levels(arg_keys[14], (D, (H + 2) * HD), ((0, 4), (1, 8)), -0.2, 0.2)), 16.384, 262.144),
        "second_out": jnp.clip(jnp.exp(math.log(262.144) - 2.7725887 * jax.random.uniform(arg_keys[15], (H * HD, D), jnp.float32) ** block_levels(arg_keys[15], (H * HD, D), ((0, 4), (1, 8)), -0.2, 0.2)), 16.384, 262.144),
        "second_gate_up": jnp.clip(jnp.exp(math.log(262.144) - 2.7725887 * jax.random.uniform(arg_keys[16], (D, 2 * FF), jnp.float32) ** block_levels(arg_keys[16], (D, 2 * FF), ((0, 4), (1, 8)), -0.2, 0.2)), 16.384, 262.144),
        "second_down": jnp.clip(jnp.exp(math.log(262.144) - 2.7725887 * jax.random.uniform(arg_keys[17], (FF, D), jnp.float32) ** block_levels(arg_keys[17], (FF, D), ((0, 4), (1, 8)), -0.2, 0.2)), 16.384, 262.144),
        "second_gains": jnp.clip(jnp.exp(math.log(262.144) - 2.7725887 * jax.random.uniform(arg_keys[18], (GAINS,), jnp.float32) ** block_levels(arg_keys[18], (GAINS,), ((0, 32),), -0.2, 0.2)), 16.384, 262.144),
    }


norm_epsilon = 1e-06
rope_base = 10000.0
beta_one = 0.9
beta_two = 0.999
adam_epsilon = 1e-08
learn_rate = 0.05
weight_decay = 0.1
neg_fill = -1e+30
block_rows = 512

@jax.custom_vjp
def low(v):
    return lax.optimization_barrier(v.astype(jnp.bfloat16)).astype(jnp.float32)

@jax.custom_vjp
def low_back(v):
    return v

def low_keep(v):
    return (low(v), None)

def low_pass(kept, grad):
    return (grad,)

def back_keep(v):
    return (v, None)

def back_low(kept, grad):
    return (low(grad),)
low.defvjp(low_keep, low_pass)
low_back.defvjp(back_keep, back_low)

def norm_apply(values, gain):
    scale = lax.rsqrt(lax.optimization_barrier(jnp.mean(values * values, axis=-1, keepdims=True)) + norm_epsilon)
    return values * scale * (1.0 + gain)

def rope_tables(positions, width):
    freqs = rope_base ** (-jnp.arange(0, width, 2).astype(jnp.float32) / width)
    angles = positions.astype(jnp.float32)[:, None] * freqs[None, :]
    return (jnp.cos(angles), jnp.sin(angles))

def rope_apply(values, cosine, sine):
    half = values.shape[-1] // 2
    first = values[..., :half]
    second = values[..., half:]
    return jnp.concatenate([first * cosine - second * sine, second * cosine + first * sine], axis=-1)

def gelu_product(gate, up):
    return jax.nn.gelu(gate, approximate=True) * up

def adam_step(grad, first, second, old, decay):
    first_new = beta_one * first + (1.0 - beta_one) * grad
    second_new = beta_two * second + (1.0 - beta_two) * grad * grad
    first_hat = first_new / (1.0 - beta_one ** STEP)
    second_hat = second_new / (1.0 - beta_two ** STEP)
    new = old - learn_rate * (first_hat / (jnp.sqrt(second_hat) + adam_epsilon) + decay * old)
    return (second_new, new)

def reference(hidden_in, cotangent, segment_ids, positions, w_qkv, w_out, w_gate_up, w_down, norm_gains, first_qkv, first_out, first_gate_up, first_down, first_gains, second_qkv, second_out, second_gate_up, second_down, second_gains):
    highest = lax.Precision.HIGHEST
    scaling = HD ** (-0.5)
    cosine, sine = rope_tables(positions, HD)
    seg_pad = jnp.concatenate([jnp.full((WINDOW,), -1, jnp.int32), segment_ids.astype(jnp.int32)])
    pos_pad = jnp.concatenate([jnp.zeros((WINDOW,), jnp.int32), positions.astype(jnp.int32)])

    def layer(inputs, weight_qkv, weight_out, weight_gate_up, weight_down, gains):
        gain_attn_in = gains[0:D]
        gain_attn_out = gains[D:2 * D]
        gain_ffn_in = gains[2 * D:3 * D]
        gain_ffn_out = gains[3 * D:4 * D]
        gain_query = gains[4 * D:4 * D + HD]
        gain_key = gains[4 * D + HD:4 * D + 2 * HD]
        attn_in = low(norm_apply(inputs, gain_attn_in))
        qkv = low_back(jnp.dot(attn_in, weight_qkv, precision=highest, preferred_element_type=jnp.float32))
        query_raw = qkv[:, :H * HD].reshape(TOKENS, H, HD)
        key_raw = qkv[:, H * HD:(H + 1) * HD]
        value_raw = qkv[:, (H + 1) * HD:]
        query = low(rope_apply(norm_apply(query_raw, gain_query), cosine[:, None, :], sine[:, None, :]))
        keys = low(rope_apply(norm_apply(key_raw, gain_key), cosine, sine))
        values = low(value_raw)
        key_pad = jnp.concatenate([jnp.zeros((WINDOW, HD), jnp.float32), keys], axis=0)
        value_pad = jnp.concatenate([jnp.zeros((WINDOW, HD), jnp.float32), values], axis=0)

        def one_block(index):
            start = index * block_rows
            block_query = lax.dynamic_slice_in_dim(query, start, block_rows, 0)
            block_key = lax.dynamic_slice_in_dim(key_pad, start, block_rows + WINDOW, 0)
            block_value = lax.dynamic_slice_in_dim(value_pad, start, block_rows + WINDOW, 0)
            seg_query = lax.dynamic_slice_in_dim(segment_ids, start, block_rows, 0)
            pos_query = lax.dynamic_slice_in_dim(positions, start, block_rows, 0)
            seg_key = lax.dynamic_slice_in_dim(seg_pad, start, block_rows + WINDOW, 0)
            pos_key = lax.dynamic_slice_in_dim(pos_pad, start, block_rows + WINDOW, 0)
            scores = low_back(scaling * jnp.einsum('thd,kd->htk', block_query, block_key, precision=highest))
            gap = pos_query[:, None] - pos_key[None, :]
            allowed = (seg_query[:, None] == seg_key[None, :]) & (gap >= 0) & (gap < WINDOW)
            masked = jnp.where(allowed[None], scores, neg_fill)
            peak = lax.optimization_barrier(jnp.max(masked, axis=-1, keepdims=True))
            expo = jnp.exp(masked - peak)
            probs = low(expo / lax.optimization_barrier(jnp.sum(expo, axis=-1, keepdims=True)))
            mixed_block = jnp.einsum('htk,kd->thd', probs, block_value, precision=highest)
            return mixed_block.reshape(block_rows, H * HD)
        mixed = lax.map(jax.checkpoint(one_block), jnp.arange(TOKENS // block_rows, dtype=jnp.int32))
        mixed = low(low_back(mixed.reshape(TOKENS, H * HD)))
        projected = low_back(jnp.dot(mixed, weight_out, precision=highest, preferred_element_type=jnp.float32))
        residual = inputs + norm_apply(projected, gain_attn_out)
        ffn_in = low(norm_apply(residual, gain_ffn_in))
        gate_up = low_back(jnp.dot(ffn_in, weight_gate_up, precision=highest, preferred_element_type=jnp.float32))
        activated = low(gelu_product(gate_up[:, :FF], gate_up[:, FF:]))
        down = low_back(jnp.dot(activated, weight_down, precision=highest, preferred_element_type=jnp.float32))
        return residual + norm_apply(down, gain_ffn_out)
    inputs = hidden_in.astype(jnp.float32)
    matrices = (w_qkv.astype(jnp.float32), w_out.astype(jnp.float32), w_gate_up.astype(jnp.float32), w_down.astype(jnp.float32))
    result, pull = jax.vjp(layer, inputs, matrices[0], matrices[1], matrices[2], matrices[3], norm_gains)
    grads = pull(cotangent.astype(jnp.float32))
    grad_qkv, grad_out, grad_gate_up, grad_down, grad_gains = (grads[1], grads[2], grads[3], grads[4], grads[5])
    moment_qkv, new_qkv = adam_step(grad_qkv, first_qkv, second_qkv, matrices[0], weight_decay)
    moment_out, new_out = adam_step(grad_out, first_out, second_out, matrices[1], weight_decay)
    moment_gate_up, new_gate_up = adam_step(grad_gate_up, first_gate_up, second_gate_up, matrices[2], weight_decay)
    moment_down, new_down = adam_step(grad_down, first_down, second_down, matrices[3], weight_decay)
    moment_gains, new_gains = adam_step(grad_gains, first_gains, second_gains, norm_gains, 0.0)
    return (result.astype(jnp.bfloat16), grads[0].astype(jnp.bfloat16), grad_qkv, grad_out, grad_gate_up, grad_down, grad_gains, moment_qkv, moment_out, moment_gate_up, moment_down, moment_gains, new_qkv, new_out, new_gate_up, new_down, new_gains)
```

```python
import functools

import jax
import jax.numpy as jnp
from jax import lax
from jax.experimental import pallas as pl
from jax.experimental.pallas import tpu as pltpu
from jax.sharding import PartitionSpec as P

MESH = pl.DeviceIdType.MESH

D = 640
H = 4
HD = 256
FF = 2048
WINDOW = 512
STEP = 10


norm_epsilon = 1e-06
rope_base = 10000.0
beta_one = 0.9
beta_two = 0.999
adam_epsilon = 1e-08
learn_rate = 0.05
weight_decay = 0.1
neg_fill = -1e30


def shifted(value, axis, by):
    peers = lax.axis_size(axis)
    pairs = [(i, i + by) for i in range(peers) if 0 <= i + by < peers]
    return lax.ppermute(value, axis, pairs)


def norm_apply(values, gain):
    scale = lax.rsqrt(jnp.mean(values * values, axis=-1, keepdims=True) + norm_epsilon)
    return values * scale * (1.0 + gain)


def rope_tables(positions, width):
    freqs = rope_base ** (-jnp.arange(0, width, 2).astype(jnp.float32) / width)
    angles = positions.astype(jnp.float32)[:, None] * freqs[None, :]
    return (jnp.cos(angles), jnp.sin(angles))


def rope_apply(values, cosine, sine):
    half = values.shape[-1] // 2
    first = values[..., :half]
    second = values[..., half:]
    return jnp.concatenate(
        [first * cosine - second * sine, second * cosine + first * sine], axis=-1
    )


def gelu_product(gate, up):
    return jax.nn.gelu(gate, approximate=True) * up


def outer_sum(left, right):
    return lax.dot_general(
        left, right, (((0,), (0,)), ((), ())), preferred_element_type=jnp.float32
    )


def back_dot(grad, weight):
    return lax.dot_general(
        grad, weight, (((1,), (1,)), ((), ())), preferred_element_type=jnp.float32
    )


def adam_step(grad, first, second, old, decay):
    first_new = beta_one * first + (1.0 - beta_one) * grad
    second_new = beta_two * second + (1.0 - beta_two) * grad * grad
    first_hat = first_new / (1.0 - beta_one**STEP)
    second_hat = second_new / (1.0 - beta_two**STEP)
    new = old - learn_rate * (first_hat / (jnp.sqrt(second_hat) + adam_epsilon) + decay * old)
    return (second_new, new)


def places():
    g = lax.axis_index("group")
    r = lax.axis_index("replica")
    core = lax.rem(r, 2)
    x = lax.rem(r // 2, 2)
    y = r // 4
    mate = r + 1 - 2 * core
    over_x = 2 - 4 * x
    over_y = 4 - 8 * y
    step_one = over_x * (1 - core) + over_y * core
    step_two = over_y * (1 - core) + over_x * core
    return g, r, mate, step_one, step_two


def meet(g, r, mate, one, two, groups):
    barrier = pltpu.get_barrier_semaphore()
    for to in (mate, one, two):
        pl.semaphore_signal(barrier, inc=1, device_id=(g, to), device_id_type=MESH)
    for far in range(1, groups):
        to = lax.rem(g + far, groups)
        pl.semaphore_signal(barrier, inc=1, device_id=(to, r), device_id_type=MESH)
    pl.semaphore_wait(barrier, 2 + groups)


def gather_kernel(groups, replicas, *refs):
    shards, fulls = refs[:4], refs[4:8]
    local_sem, a_send, a_recv, b_send, b_recv = refs[8:]
    g, r, mate, step_one, step_two = places()
    one, two = r + step_one, r + step_two
    diagonal = r + step_one + step_two
    chips = replicas // 2

    def view(ref, which, height, base, index):
        width = ref.shape[1]
        if which == 0:
            rows = height // 2
            part = width // chips
            return ref.at[
                pl.ds(pl.multiple_of(base + lax.rem(index, 2) * rows, 16), rows),
                pl.ds(pl.multiple_of((index // 2) * part, 128), part),
            ]
        if which == 2:
            part = width // replicas
            return ref.at[
                pl.ds(pl.multiple_of(base, 16), height),
                pl.ds(pl.multiple_of(index * part, 128), part),
            ]
        rows = height // replicas
        return ref.at[pl.ds(pl.multiple_of(base + index * rows, 16), rows), :]

    def place(which, group, index):
        height = shards[which].shape[0]
        return view(fulls[which], which, height, group * height, index)

    def send(src, dst, send_sem, recv_sem, to):
        return pltpu.make_async_remote_copy(
            src_ref=src, dst_ref=dst, send_sem=send_sem, recv_sem=recv_sem,
            device_id=to, device_id_type=MESH,
        )

    meet(g, r, mate, one, two, groups)
    started = []
    items = [(which, far) for which in range(4) for far in range(1, groups)]
    for which, far in items:
        shard = shards[which]
        copy = send(
            view(shard, which, shard.shape[0], 0, r),
            place(which, g, r),
            a_send.at[far - 1, which],
            a_recv.at[far - 1, which],
            (lax.rem(g + far, groups), r),
        )
        copy.start()
        started.append(copy)
    own = []
    for which in range(4):
        height = shards[which].shape[0]
        copy = pltpu.make_async_copy(
            shards[which],
            fulls[which].at[pl.ds(pl.multiple_of(g * height, 16), height), :],
            local_sem.at[which],
        )
        copy.start()
        own.append(copy)

    def push(item, slot, index, to):
        which, far = items[item]
        part = place(which, lax.rem(g + groups - far, groups), index)
        copy = send(part, part, b_send.at[item, slot], b_recv.at[item, slot], (g, to))
        copy.start()
        started.append(copy)

    def arrived(item, slot, index):
        which, far = items[item]
        part = place(which, lax.rem(g + groups - far, groups), index)
        send(part, part, b_send.at[item, slot], b_recv.at[item, slot], (g, mate)).wait_recv()

    for turn in range(len(items) + 2):
        if turn < len(items):
            which, far = items[turn]
            part = place(which, lax.rem(g + groups - far, groups), r)
            send(
                part, part, a_send.at[far - 1, which], a_recv.at[far - 1, which], (g, mate)
            ).wait_recv()
            push(turn, 0, r, one)
            push(turn, 1, r, two)
            push(turn, 3, r, mate)
        item = turn - 1
        if 0 <= item < len(items):
            arrived(item, 0, one)
            push(item, 2, one, two)
            push(item, 4, one, mate)
        item = turn - 2
        if 0 <= item < len(items):
            arrived(item, 1, two)
            push(item, 5, two, mate)
            arrived(item, 2, diagonal)
            push(item, 6, diagonal, mate)
    for item in range(len(items)):
        arrived(item, 3, mate)
        arrived(item, 4, mate + step_two)
        arrived(item, 5, mate + step_one)
        arrived(item, 6, mate + step_one + step_two)
    for copy in own:
        copy.wait()
    for copy in started:
        copy.wait_send()


def gather_weights(groups, replicas, *shards):
    items = 4 * (groups - 1)
    dma = pltpu.SemaphoreType.DMA
    return pl.pallas_call(
        functools.partial(gather_kernel, groups, replicas),
        out_shape=[
            jax.ShapeDtypeStruct((groups * s.shape[0], s.shape[1]), s.dtype) for s in shards
        ],
        in_specs=[pl.BlockSpec(memory_space=pl.ANY)] * 4,
        out_specs=[pl.BlockSpec(memory_space=pl.ANY)] * 4,
        scratch_shapes=[
            dma((4,)),
            dma((groups - 1, 4)),
            dma((groups - 1, 4)),
            dma((items, 7)),
            dma((items, 7)),
        ],
        compiler_params=pltpu.CompilerParams(collective_id=1, has_side_effects=True),
        cost_estimate=pl.CostEstimate(flops=0, bytes_accessed=25000000, transcendentals=0),
        name="gather_weights",
    )(*shards)


lanes = 128


def sum_kernel(groups, replicas, dims, *refs):
    (at, dqkv, bt, dgu, dzt, o, dmt, f, gains) = refs[:9]
    out_q, out_g, out_o, out_d, out_n = refs[9:14]
    to_mate, kept, from_mate, from_one, from_two, from_far = refs[14:20]
    c_send, c_recv, x_send, x_recv, y_send, y_recv, z_send, z_recv = refs[20:]
    rows_in, q_wide, g_wide, thin, o_wide, d_wide, rows = dims
    g, r, mate, step_one, step_two = places()
    one, two = r + step_one, r + step_two

    def dot(left, right):
        return jnp.dot(left, right, preferred_element_type=jnp.float32).astype(jnp.bfloat16)

    def compute(dst, group, index):
        top = pl.ds(pl.multiple_of(group * rows_in, 16), rows_in)
        side = pl.ds(pl.multiple_of(index * thin, 16), thin)

        def columns(width, place):
            return pl.ds(pl.multiple_of(place * width, 128), width)

        at_row = 0
        for left, right, height, width in (
            (at[top, :], dqkv[:, columns(q_wide, index)], rows_in, q_wide),
            (bt[top, :], dgu[:, columns(g_wide, index)], rows_in, g_wide),
            (dzt[side, :], o[:, columns(o_wide, group)], thin, o_wide),
            (dmt[side, :], f[:, columns(d_wide, group)], thin, d_wide),
        ):
            block = dot(left, right)
            for stripe in range(width // lanes):
                dst[pl.ds(at_row, height), :] = block[:, stripe * lanes : (stripe + 1) * lanes]
                at_row += height
        dst[pl.ds(at_row, 16), :] = gains[index, group]

    def send(src, dst, send_sem, recv_sem, to):
        return pltpu.make_async_remote_copy(
            src_ref=src, dst_ref=dst, send_sem=send_sem, recv_sem=recv_sem,
            device_id=to, device_id_type=MESH,
        )

    def add(dst, src):
        part = 208
        def body(i, carry):
            here = pl.ds(pl.multiple_of(i * part, 16), part)
            dst[here, :] = (
                dst[here, :].astype(jnp.float32) + src[here, :].astype(jnp.float32)
            ).astype(jnp.bfloat16)
            return carry
        lax.fori_loop(0, rows // part, body, 0)

    def flips(m):
        return 1 - m // 2, lax.rem((m + 1) // 2, 2)

    def target(stage):
        return lax.rem(g + 1 + stage, groups)

    def mate_copy(stage, m):
        return send(
            to_mate.at[stage, m], from_mate.at[stage, m], c_send.at[stage, m], c_recv.at[stage, m],
            (g, mate),
        )

    def one_copy(stage, m):
        return send(
            kept.at[stage, m], from_one.at[stage, 1 - m], x_send.at[stage, 1 - m],
            x_recv.at[stage, 1 - m], (g, one),
        )

    def two_copy(stage):
        return send(
            kept.at[stage, 2], from_two.at[stage], y_send.at[stage], y_recv.at[stage], (g, two)
        )

    def far_copy(stage):
        return send(
            kept.at[stage, 3], from_far.at[stage], z_send.at[stage], z_recv.at[stage],
            (target(stage), r),
        )

    def make(stage):
        def for_mate(m, carry):
            first, second = flips(m)
            compute(
                to_mate.at[stage, m], target(stage), mate + first * step_two + second * step_one
            )
            mate_copy(stage, m).start()
            return carry

        def for_me(m, carry):
            first, second = flips(m)
            compute(kept.at[stage, m], target(stage), r + first * step_one + second * step_two)
            return carry

        lax.fori_loop(0, 4, for_mate, 0)
        lax.fori_loop(0, 4, for_me, 0)

    def pass_one(stage):
        for m in (1, 0):
            mate_copy(stage, m).wait_recv()
            add(kept.at[stage, m], from_mate.at[stage, m])
            one_copy(stage, m).start()
        for m in (2, 3):
            mate_copy(stage, m).wait_recv()
            add(kept.at[stage, m], from_mate.at[stage, m])

    def pass_two(stage):
        one_copy(stage, 1).wait_recv()
        add(kept.at[stage, 2], from_one.at[stage, 0])
        two_copy(stage).start()
        one_copy(stage, 0).wait_recv()
        add(kept.at[stage, 3], from_one.at[stage, 1])

    def pass_far(stage):
        two_copy(stage).wait_recv()
        add(kept.at[stage, 3], from_two.at[stage])
        if stage < groups - 1:
            far_copy(stage).start()

    meet(g, r, mate, one, two, groups)
    for turn in range(groups + 3):
        if turn < groups:
            make(turn)
        if 0 <= turn - 1 < groups:
            pass_one(turn - 1)
        if 0 <= turn - 2 < groups:
            pass_two(turn - 2)
        if 0 <= turn - 3 < groups:
            pass_far(turn - 3)
    for stage in range(groups - 1):
        far_copy(stage).wait_recv()
    at_row = 0
    for out, height, width in (
        (out_q, rows_in, q_wide),
        (out_g, rows_in, g_wide),
        (out_o, thin, o_wide),
        (out_d, thin, d_wide),
        (out_n, 16, lanes),
    ):
        for stripe in range(width // lanes):
            here = pl.ds(at_row, height)
            total = kept[groups - 1, 3, here, :].astype(jnp.float32)
            for stage in range(groups - 1):
                total = total + from_far[stage, here, :].astype(jnp.float32)
            out[:, stripe * lanes : (stripe + 1) * lanes] = total
            at_row += height
    for stage in range(groups):
        for m in range(4):
            mate_copy(stage, m).wait_send()
        for m in range(2):
            one_copy(stage, m).wait_send()
        two_copy(stage).wait_send()
        if stage < groups - 1:
            far_copy(stage).wait_send()


def sum_gradients(groups, replicas, attn_in, d_qkv, ffn_in, d_gate_up, d_proj, mixed, d_down, act, gain_terms):
    tokens = attn_in.shape[0]
    rows_in = D // groups
    thin = D // replicas
    q_part = d_qkv.shape[1] // replicas
    q_wide = -(-q_part // lanes) * lanes
    g_wide = d_gate_up.shape[1] // replicas
    o_wide = mixed.shape[1] // groups
    d_wide = act.shape[1] // groups
    d_qkv = jnp.pad(d_qkv.reshape(tokens, replicas, q_part), ((0, 0), (0, 0), (0, q_wide - q_part)))
    d_qkv = d_qkv.reshape(tokens, replicas * q_wide)
    share = gain_terms.shape[0] // (groups * replicas)
    gains = gain_terms.reshape(groups, replicas, 1, share).transpose(1, 0, 2, 3)
    gains = jnp.pad(gains, ((0, 0), (0, 0), (0, 15), (0, lanes - share))).astype(jnp.bfloat16)
    rows = (rows_in * (q_wide + g_wide) + thin * (o_wide + d_wide)) // lanes + 16
    dims = (rows_in, q_wide, g_wide, thin, o_wide, d_wide, rows)
    dma = pltpu.SemaphoreType.DMA
    vmem = pl.BlockSpec(memory_space=pltpu.VMEM)
    f32 = jnp.float32
    got = pl.pallas_call(
        functools.partial(sum_kernel, groups, replicas, dims),
        out_shape=[
            jax.ShapeDtypeStruct((rows_in, q_wide), f32),
            jax.ShapeDtypeStruct((rows_in, g_wide), f32),
            jax.ShapeDtypeStruct((thin, o_wide), f32),
            jax.ShapeDtypeStruct((thin, d_wide), f32),
            jax.ShapeDtypeStruct((16, lanes), f32),
        ],
        in_specs=[vmem] * 9,
        out_specs=[vmem] * 5,
        scratch_shapes=[
            pltpu.VMEM((groups, 4, rows, lanes), jnp.bfloat16),
            pltpu.VMEM((groups, 4, rows, lanes), jnp.bfloat16),
            pltpu.VMEM((groups, 4, rows, lanes), jnp.bfloat16),
            pltpu.VMEM((groups, 2, rows, lanes), jnp.bfloat16),
            pltpu.VMEM((groups, rows, lanes), jnp.bfloat16),
            pltpu.VMEM((groups - 1, rows, lanes), jnp.bfloat16),
            dma((groups, 4)), dma((groups, 4)),
            dma((groups, 2)), dma((groups, 2)),
            dma((groups,)), dma((groups,)),
            dma((groups - 1,)), dma((groups - 1,)),
        ],
        compiler_params=pltpu.CompilerParams(
            collective_id=2, has_side_effects=True, vmem_limit_bytes=48 * 1024 * 1024
        ),
        cost_estimate=pl.CostEstimate(flops=3000000000, bytes_accessed=12000000, transcendentals=0),
        name="sum_gradients",
    )(attn_in.T, d_qkv, ffn_in.T, d_gate_up, d_proj.T, mixed, d_down.T, act, gains)
    return (got[0][:, :q_part], got[2].T, got[1], got[3].T, got[4][0, :share])


def body(
    hidden_in,
    cotangent,
    segment_ids,
    positions,
    w_qkv,
    w_out,
    w_gate_up,
    w_down,
    norm_gains,
    first_qkv,
    first_out,
    first_gate_up,
    first_down,
    first_gains,
    second_qkv,
    second_out,
    second_gate_up,
    second_down,
    second_gains,
):
    tokens = hidden_in.shape[0]
    scaling = HD ** (-0.5)
    groups = lax.axis_size("group")
    replicas = lax.axis_size("replica")
    direct = (groups, replicas) == (4, 8)
    if direct:
        full_qkv, full_out, full_gate_up, full_down = gather_weights(
            groups, replicas, w_qkv, w_out, w_gate_up, w_down
        )
    else:
        full_qkv, full_out, full_gate_up, full_down = (
            lax.all_gather(w_qkv, "group", axis=0, tiled=True),
            lax.all_gather(w_out, "group", axis=0, tiled=True),
            lax.all_gather(w_gate_up, "group", axis=0, tiled=True),
            lax.all_gather(w_down, "group", axis=0, tiled=True),
        )
    gain_attn_in = norm_gains[0:D]
    gain_attn_out = norm_gains[D : 2 * D]
    gain_ffn_in = norm_gains[2 * D : 3 * D]
    gain_ffn_out = norm_gains[3 * D : 4 * D]
    gain_query = norm_gains[4 * D : 4 * D + HD]
    gain_key = norm_gains[4 * D + HD : 4 * D + 2 * HD]
    cosine, sine = rope_tables(positions, HD)

    def query_key(query_raw, key_raw, gain_q, gain_k):
        query_rot = rope_apply(norm_apply(query_raw, gain_q), cosine[:, None, :], sine[:, None, :])
        key_rot = rope_apply(norm_apply(key_raw, gain_k), cosine, sine)
        return (query_rot, key_rot)

    inputs = hidden_in.astype(jnp.float32)
    attn_in = norm_apply(inputs, gain_attn_in).astype(jnp.bfloat16)
    qkv = jnp.dot(attn_in, full_qkv, preferred_element_type=jnp.float32)
    query_raw = qkv[:, : H * HD].reshape(tokens, H, HD)
    key_raw = qkv[:, H * HD : (H + 1) * HD]
    value_raw = qkv[:, (H + 1) * HD :]
    query_rot, key_rot = query_key(query_raw, key_raw, gain_query, gain_key)
    query_low = query_rot.astype(jnp.bfloat16)
    keyval = jnp.concatenate([key_rot.astype(jnp.bfloat16), value_raw.astype(jnp.bfloat16)], axis=1)
    own_ids = jnp.stack([segment_ids + 1, positions])
    reaches = -(-WINDOW // tokens)
    key_parts = [keyval]
    id_parts = [own_ids]
    for reach in range(1, reaches + 1):
        key_parts.insert(0, shifted(keyval, ("group", "replica"), reach))
        id_parts.insert(0, shifted(own_ids, ("group", "replica"), reach))
    key_all = jnp.concatenate(key_parts, axis=0)
    ids_all = jnp.concatenate(id_parts, axis=1)
    key_low = key_all[:, :HD]
    value_low = key_all[:, HD:]
    gap = positions[:, None] - ids_all[1][None, :]
    allowed = (ids_all[0][None, :] == (segment_ids + 1)[:, None]) & (gap >= 0) & (gap < WINDOW)

    def masked_scores():
        scores = (
            jnp.einsum("thd,kd->htk", query_low, key_low, preferred_element_type=jnp.float32)
            * scaling
        )
        return jnp.where(allowed[None], scores, neg_fill)

    masked = masked_scores()
    peak = jnp.max(masked, axis=-1, keepdims=True)
    expo = jnp.exp(masked - peak)
    total = jnp.sum(expo, axis=-1, keepdims=True)
    probs_low = (expo / total).astype(jnp.bfloat16)
    mixed = jnp.einsum("htk,kd->thd", probs_low, value_low, preferred_element_type=jnp.float32)
    mixed_low = mixed.reshape(tokens, H * HD).astype(jnp.bfloat16)
    projected = jnp.dot(mixed_low, full_out, preferred_element_type=jnp.float32)
    residual = inputs + norm_apply(projected, gain_attn_out)
    ffn_in = norm_apply(residual, gain_ffn_in).astype(jnp.bfloat16)
    gate_up = jnp.dot(ffn_in, full_gate_up, preferred_element_type=jnp.float32)
    activated = gelu_product(gate_up[:, :FF], gate_up[:, FF:]).astype(jnp.bfloat16)
    down = jnp.dot(activated, full_down, preferred_element_type=jnp.float32)
    block_out = (residual + norm_apply(down, gain_ffn_out)).astype(jnp.bfloat16)
    upstream = cotangent.astype(jnp.float32)
    unused, pull = jax.vjp(norm_apply, down, gain_ffn_out)
    d_down, grad_ffn_out = pull(upstream)
    d_down_low = d_down.astype(jnp.bfloat16)
    d_activated = back_dot(d_down_low, full_down)
    unused, pull = jax.vjp(gelu_product, gate_up[:, :FF], gate_up[:, FF:])
    d_gate, d_up = pull(d_activated)
    d_gate_up_low = jnp.concatenate([d_gate, d_up], axis=1).astype(jnp.bfloat16)
    d_ffn_in = back_dot(d_gate_up_low, full_gate_up)
    unused, pull = jax.vjp(norm_apply, residual, gain_ffn_in)
    d_residual_ffn, grad_ffn_in = pull(d_ffn_in)
    d_residual = upstream + d_residual_ffn
    unused, pull = jax.vjp(norm_apply, projected, gain_attn_out)
    d_projected, grad_attn_out = pull(d_residual)
    d_projected_low = d_projected.astype(jnp.bfloat16)
    d_mixed_low = back_dot(d_projected_low, full_out).astype(jnp.bfloat16).reshape(tokens, H, HD)
    probs_again = jnp.exp(masked_scores() - peak) / total
    d_probs = jnp.einsum("thd,kd->htk", d_mixed_low, value_low, preferred_element_type=jnp.float32)
    d_scores = probs_again * (d_probs - jnp.sum(d_probs * probs_again, axis=-1, keepdims=True))
    d_scores_low = d_scores.astype(jnp.bfloat16)
    d_query = (
        jnp.einsum("htk,kd->thd", d_scores_low, key_low, preferred_element_type=jnp.float32)
        * scaling
    )
    d_keys = (
        jnp.einsum("htk,thd->kd", d_scores_low, query_low, preferred_element_type=jnp.float32)
        * scaling
    )
    d_values = jnp.einsum("htk,thd->kd", probs_low, d_mixed_low, preferred_element_type=jnp.float32)
    key_grads = jnp.concatenate([d_keys, d_values], axis=1)
    own_grads = key_grads[reaches * tokens :]
    for reach in range(1, reaches + 1):
        piece = key_grads[(reaches - reach) * tokens : (reaches - reach + 1) * tokens]
        own_grads = own_grads + shifted(
            piece.astype(jnp.bfloat16), ("group", "replica"), -reach
        ).astype(piece.dtype)
    unused, pull = jax.vjp(query_key, query_raw, key_raw, gain_query, gain_key)
    d_query_raw, d_key_raw, grad_query, grad_key = pull((d_query, own_grads[:, :HD]))
    d_qkv_low = jnp.concatenate(
        [d_query_raw.reshape(tokens, H * HD), d_key_raw, own_grads[:, HD:]], axis=1
    ).astype(jnp.bfloat16)
    d_attn_in = back_dot(d_qkv_low, full_qkv)
    unused, pull = jax.vjp(norm_apply, inputs, gain_attn_in)
    d_inputs, grad_attn_in = pull(d_attn_in)
    grad_in = (d_residual + d_inputs).astype(jnp.bfloat16)
    gain_terms = jnp.concatenate(
        [grad_attn_in, grad_attn_out, grad_ffn_in, grad_ffn_out, grad_query, grad_key]
    )
    column = lax.axis_index("replica")
    if direct:
        owned = sum_gradients(
            groups, replicas, attn_in, d_qkv_low, ffn_in, d_gate_up_low, d_projected_low,
            mixed_low, d_down_low, activated, gain_terms,
        )
    else:
        gain_rows = gain_terms.reshape(groups, gain_terms.shape[0] // groups)
        terms = (
            outer_sum(attn_in, d_qkv_low),
            outer_sum(mixed_low, d_projected_low),
            outer_sum(ffn_in, d_gate_up_low),
            outer_sum(activated, d_down_low),
            gain_rows,
        )
        row_sums = (
            lax.psum_scatter(
                terms[0].astype(jnp.bfloat16), "group", scatter_dimension=0, tiled=True
            ).astype(jnp.float32),
            lax.psum_scatter(
                terms[1].astype(jnp.bfloat16), "group", scatter_dimension=0, tiled=True
            ).astype(jnp.float32),
            lax.psum_scatter(
                terms[2].astype(jnp.bfloat16), "group", scatter_dimension=0, tiled=True
            ).astype(jnp.float32),
            lax.psum_scatter(
                terms[3].astype(jnp.bfloat16), "group", scatter_dimension=0, tiled=True
            ).astype(jnp.float32),
            lax.psum_scatter(
                terms[4].astype(jnp.bfloat16), "group", scatter_dimension=0, tiled=True
            ).astype(jnp.float32),
        )
        totals = lax.psum((row_sums[0], row_sums[1], row_sums[2], row_sums[3], row_sums[4]), "replica")
        owned = tuple(
            (
                lax.dynamic_slice_in_dim(
                    item, column * (item.shape[1] // replicas), item.shape[1] // replicas, 1
                )
                for item in totals
            )
        )
        owned = owned[:4] + (owned[4].reshape(-1),)

    def old_columns(weight):
        width = weight.shape[1] // replicas
        return lax.dynamic_slice_in_dim(weight, column * width, width, 1).astype(jnp.float32)

    moment_qkv, new_qkv = adam_step(
        owned[0], first_qkv, second_qkv, old_columns(w_qkv), weight_decay
    )
    moment_out, new_out = adam_step(
        owned[1], first_out, second_out, old_columns(w_out), weight_decay
    )
    moment_gate_up, new_gate_up = adam_step(
        owned[2], first_gate_up, second_gate_up, old_columns(w_gate_up), weight_decay
    )
    moment_down, new_down = adam_step(
        owned[3], first_down, second_down, old_columns(w_down), weight_decay
    )
    grad_gains = owned[4]
    share = grad_gains.shape[0]
    owner = lax.axis_index("group") * replicas + column
    old_gains = lax.dynamic_slice_in_dim(norm_gains, owner * share, share, 0)
    moment_gains, new_gains = adam_step(grad_gains, first_gains, second_gains, old_gains, 0.0)
    return (
        block_out,
        grad_in,
        owned[0],
        owned[1],
        owned[2],
        owned[3],
        grad_gains,
        moment_qkv,
        moment_out,
        moment_gate_up,
        moment_down,
        moment_gains,
        new_qkv,
        new_out,
        new_gate_up,
        new_down,
        new_gains,
    )


def solution(mesh):
    in_specs = (
        P(("group", "replica"), None),
        P(("group", "replica"), None),
        P(("group", "replica")),
        P(("group", "replica")),
        P("group", None),
        P("group", None),
        P("group", None),
        P("group", None),
        P(),
        P("group", "replica"),
        P("group", "replica"),
        P("group", "replica"),
        P("group", "replica"),
        P(("group", "replica")),
        P("group", "replica"),
        P("group", "replica"),
        P("group", "replica"),
        P("group", "replica"),
        P(("group", "replica")),
    )
    out_specs = (
        P(("group", "replica"), None),
        P(("group", "replica"), None),
        P("group", "replica"),
        P("group", "replica"),
        P("group", "replica"),
        P("group", "replica"),
        P(("group", "replica")),
        P("group", "replica"),
        P("group", "replica"),
        P("group", "replica"),
        P("group", "replica"),
        P(("group", "replica")),
        P("group", "replica"),
        P("group", "replica"),
        P("group", "replica"),
        P("group", "replica"),
        P(("group", "replica")),
    )
    return jax.shard_map(body, mesh=mesh, in_specs=in_specs, out_specs=out_specs, check_vma=False)
```

```python
import functools

import jax
import jax.numpy as jnp
from jax import lax
from jax.experimental import pallas as pl
from jax.experimental.pallas import tpu as pltpu
from jax.sharding import PartitionSpec as P

MESH = pl.DeviceIdType.MESH

D = 640
H = 4
HD = 256
FF = 2048
WINDOW = 512
STEP = 10


norm_epsilon = 1e-06
rope_base = 10000.0
beta_one = 0.9
beta_two = 0.999
adam_epsilon = 1e-08
learn_rate = 0.05
weight_decay = 0.1
neg_fill = -1e30


def shifted(value, axis, by):
    peers = lax.axis_size(axis)
    pairs = [(i, i + by) for i in range(peers) if 0 <= i + by < peers]
    return lax.ppermute(value, axis, pairs)


def norm_apply(values, gain):
    scale = lax.rsqrt(jnp.mean(values * values, axis=-1, keepdims=True) + norm_epsilon)
    return values * scale * (1.0 + gain)


def rope_tables(positions, width):
    freqs = rope_base ** (-jnp.arange(0, width, 2).astype(jnp.float32) / width)
    angles = positions.astype(jnp.float32)[:, None] * freqs[None, :]
    return (jnp.cos(angles), jnp.sin(angles))


def rope_apply(values, cosine, sine):
    half = values.shape[-1] // 2
    first = values[..., :half]
    second = values[..., half:]
    return jnp.concatenate(
        [first * cosine - second * sine, second * cosine + first * sine], axis=-1
    )


def gelu_product(gate, up):
    return jax.nn.gelu(gate, approximate=True) * up


def outer_sum(left, right):
    return lax.dot_general(
        left, right, (((0,), (0,)), ((), ())), preferred_element_type=jnp.float32
    )


def back_dot(grad, weight):
    return lax.dot_general(
        grad, weight, (((1,), (1,)), ((), ())), preferred_element_type=jnp.float32
    )


def adam_step(grad, first, second, old, decay):
    first_new = beta_one * first + (1.0 - beta_one) * grad
    second_new = beta_two * second + (1.0 - beta_two) * grad * grad
    first_hat = first_new / (1.0 - beta_one**STEP)
    second_hat = second_new / (1.0 - beta_two**STEP)
    new = old - learn_rate * (first_hat / (jnp.sqrt(second_hat) + adam_epsilon) + decay * old)
    return (second_new, new)


def places():
    g = lax.axis_index("group")
    r = lax.axis_index("replica")
    core = lax.rem(r, 2)
    x = lax.rem(r // 2, 2)
    y = r // 4
    mate = r + 1 - 2 * core
    over_x = 2 - 4 * x
    over_y = 4 - 8 * y
    step_one = over_x * (1 - core) + over_y * core
    step_two = over_y * (1 - core) + over_x * core
    return g, r, mate, step_one, step_two


def meet(g, r, mate, one, two, groups):
    barrier = pltpu.get_barrier_semaphore()
    for to in (mate, one, two):
        pl.semaphore_signal(barrier, inc=1, device_id=(g, to), device_id_type=MESH)
    for far in range(1, groups):
        to = lax.rem(g + far, groups)
        pl.semaphore_signal(barrier, inc=1, device_id=(to, r), device_id_type=MESH)
    pl.semaphore_wait(barrier, 2 + groups)


def gather_kernel(groups, replicas, *refs):
    shards, fulls = refs[:4], refs[4:8]
    local_sem, a_send, a_recv, b_send, b_recv = refs[8:]
    g, r, mate, step_one, step_two = places()
    one, two = r + step_one, r + step_two
    diagonal = r + step_one + step_two
    chips = replicas // 2

    def view(ref, which, height, base, index):
        width = ref.shape[1]
        if which == 0:
            rows = height // 2
            part = width // chips
            return ref.at[
                pl.ds(pl.multiple_of(base + lax.rem(index, 2) * rows, 16), rows),
                pl.ds(pl.multiple_of((index // 2) * part, 128), part),
            ]
        if which == 2:
            part = width // replicas
            return ref.at[
                pl.ds(pl.multiple_of(base, 16), height),
                pl.ds(pl.multiple_of(index * part, 128), part),
            ]
        rows = height // replicas
        return ref.at[pl.ds(pl.multiple_of(base + index * rows, 16), rows), :]

    def place(which, group, index):
        height = shards[which].shape[0]
        return view(fulls[which], which, height, group * height, index)

    def send(src, dst, send_sem, recv_sem, to):
        return pltpu.make_async_remote_copy(
            src_ref=src, dst_ref=dst, send_sem=send_sem, recv_sem=recv_sem,
            device_id=to, device_id_type=MESH,
        )

    meet(g, r, mate, one, two, groups)
    started = []
    items = [(which, far) for which in range(4) for far in range(1, groups)]
    for which, far in items:
        shard = shards[which]
        copy = send(
            view(shard, which, shard.shape[0], 0, r),
            place(which, g, r),
            a_send.at[far - 1, which],
            a_recv.at[far - 1, which],
            (lax.rem(g + far, groups), r),
        )
        copy.start()
        started.append(copy)
    own = []
    for which in range(4):
        height = shards[which].shape[0]
        copy = pltpu.make_async_copy(
            shards[which],
            fulls[which].at[pl.ds(pl.multiple_of(g * height, 16), height), :],
            local_sem.at[which],
        )
        copy.start()
        own.append(copy)

    def push(item, slot, index, to):
        which, far = items[item]
        part = place(which, lax.rem(g + groups - far, groups), index)
        copy = send(part, part, b_send.at[item, slot], b_recv.at[item, slot], (g, to))
        copy.start()
        started.append(copy)

    def arrived(item, slot, index):
        which, far = items[item]
        part = place(which, lax.rem(g + groups - far, groups), index)
        send(part, part, b_send.at[item, slot], b_recv.at[item, slot], (g, mate)).wait_recv()

    for turn in range(len(items) + 2):
        if turn < len(items):
            which, far = items[turn]
            part = place(which, lax.rem(g + groups - far, groups), r)
            send(
                part, part, a_send.at[far - 1, which], a_recv.at[far - 1, which], (g, mate)
            ).wait_recv()
            push(turn, 0, r, one)
            push(turn, 1, r, two)
            push(turn, 3, r, mate)
        item = turn - 1
        if 0 <= item < len(items):
            arrived(item, 0, one)
            push(item, 2, one, two)
            push(item, 4, one, mate)
        item = turn - 2
        if 0 <= item < len(items):
            arrived(item, 1, two)
            push(item, 5, two, mate)
            arrived(item, 2, diagonal)
            push(item, 6, diagonal, mate)
    for item in range(len(items)):
        arrived(item, 3, mate)
        arrived(item, 4, mate + step_two)
        arrived(item, 5, mate + step_one)
        arrived(item, 6, mate + step_one + step_two)
    for copy in own:
        copy.wait()
    for copy in started:
        copy.wait_send()


def gather_weights(groups, replicas, *shards):
    items = 4 * (groups - 1)
    dma = pltpu.SemaphoreType.DMA
    return pl.pallas_call(
        functools.partial(gather_kernel, groups, replicas),
        out_shape=[
            jax.ShapeDtypeStruct((groups * s.shape[0], s.shape[1]), s.dtype) for s in shards
        ],
        in_specs=[pl.BlockSpec(memory_space=pltpu.VMEM)] * 4,
        out_specs=[pl.BlockSpec(memory_space=pltpu.VMEM)] * 4,
        scratch_shapes=[
            dma((4,)),
            dma((groups - 1, 4)),
            dma((groups - 1, 4)),
            dma((items, 7)),
            dma((items, 7)),
        ],
        compiler_params=pltpu.CompilerParams(
            collective_id=1, has_side_effects=True, vmem_limit_bytes=48 * 1024 * 1024
        ),
        cost_estimate=pl.CostEstimate(flops=0, bytes_accessed=25000000, transcendentals=0),
        name="gather_weights",
    )(*shards)


lanes = 128


def sum_kernel(groups, replicas, dims, *refs):
    (at, dqkv, bt, dgu, dzt, o, dmt, f, gains) = refs[:9]
    out_q, out_g, out_o, out_d, out_n = refs[9:14]
    to_mate, kept, from_mate, from_one, from_two, from_far = refs[14:20]
    c_send, c_recv, x_send, x_recv, y_send, y_recv, z_send, z_recv = refs[20:]
    rows_in, q_wide, g_wide, thin, o_wide, d_wide, rows = dims
    g, r, mate, step_one, step_two = places()
    one, two = r + step_one, r + step_two

    def dot(left, right):
        return jnp.dot(left, right, preferred_element_type=jnp.float32).astype(jnp.bfloat16)

    def compute(dst, group, index):
        top = pl.ds(pl.multiple_of(group * rows_in, 16), rows_in)
        side = pl.ds(pl.multiple_of(index * thin, 16), thin)

        def columns(width, place):
            return pl.ds(pl.multiple_of(place * width, 128), width)

        at_row = 0
        for left, right, height, width in (
            (at[top, :], dqkv[:, columns(q_wide, index)], rows_in, q_wide),
            (bt[top, :], dgu[:, columns(g_wide, index)], rows_in, g_wide),
            (dzt[side, :], o[:, columns(o_wide, group)], thin, o_wide),
            (dmt[side, :], f[:, columns(d_wide, group)], thin, d_wide),
        ):
            block = dot(left, right)
            for stripe in range(width // lanes):
                dst[pl.ds(at_row, height), :] = block[:, stripe * lanes : (stripe + 1) * lanes]
                at_row += height
        dst[pl.ds(at_row, 16), :] = gains[index, group]

    def send(src, dst, send_sem, recv_sem, to):
        return pltpu.make_async_remote_copy(
            src_ref=src, dst_ref=dst, send_sem=send_sem, recv_sem=recv_sem,
            device_id=to, device_id_type=MESH,
        )

    def add(dst, src):
        part = 208
        def body(i, carry):
            here = pl.ds(pl.multiple_of(i * part, 16), part)
            dst[here, :] = (
                dst[here, :].astype(jnp.float32) + src[here, :].astype(jnp.float32)
            ).astype(jnp.bfloat16)
            return carry
        lax.fori_loop(0, rows // part, body, 0)

    def flips(m):
        return 1 - m // 2, lax.rem((m + 1) // 2, 2)

    def target(stage):
        return lax.rem(g + 1 + stage, groups)

    def mate_copy(stage, m):
        return send(
            to_mate.at[stage, m], from_mate.at[stage, m], c_send.at[stage, m], c_recv.at[stage, m],
            (g, mate),
        )

    def one_copy(stage, m):
        return send(
            kept.at[stage, m], from_one.at[stage, 1 - m], x_send.at[stage, 1 - m],
            x_recv.at[stage, 1 - m], (g, one),
        )

    def two_copy(stage):
        return send(
            kept.at[stage, 2], from_two.at[stage], y_send.at[stage], y_recv.at[stage], (g, two)
        )

    def far_copy(stage):
        return send(
            kept.at[stage, 3], from_far.at[stage], z_send.at[stage], z_recv.at[stage],
            (target(stage), r),
        )

    def make(stage):
        def for_mate(m, carry):
            first, second = flips(m)
            compute(
                to_mate.at[stage, m], target(stage), mate + first * step_two + second * step_one
            )
            mate_copy(stage, m).start()
            return carry

        def for_me(m, carry):
            first, second = flips(m)
            compute(kept.at[stage, m], target(stage), r + first * step_one + second * step_two)
            return carry

        lax.fori_loop(0, 4, for_mate, 0)
        lax.fori_loop(0, 4, for_me, 0)

    def pass_one(stage):
        for m in (1, 0):
            mate_copy(stage, m).wait_recv()
            add(kept.at[stage, m], from_mate.at[stage, m])
            one_copy(stage, m).start()
        for m in (2, 3):
            mate_copy(stage, m).wait_recv()
            add(kept.at[stage, m], from_mate.at[stage, m])

    def pass_two(stage):
        one_copy(stage, 1).wait_recv()
        add(kept.at[stage, 2], from_one.at[stage, 0])
        two_copy(stage).start()
        one_copy(stage, 0).wait_recv()
        add(kept.at[stage, 3], from_one.at[stage, 1])

    def pass_far(stage):
        two_copy(stage).wait_recv()
        add(kept.at[stage, 3], from_two.at[stage])
        if stage < groups - 1:
            far_copy(stage).start()

    meet(g, r, mate, one, two, groups)
    for turn in range(groups + 3):
        if turn < groups:
            make(turn)
        if 0 <= turn - 1 < groups:
            pass_one(turn - 1)
        if 0 <= turn - 2 < groups:
            pass_two(turn - 2)
        if 0 <= turn - 3 < groups:
            pass_far(turn - 3)
    for stage in range(groups - 1):
        far_copy(stage).wait_recv()
    at_row = 0
    for out, height, width in (
        (out_q, rows_in, q_wide),
        (out_g, rows_in, g_wide),
        (out_o, thin, o_wide),
        (out_d, thin, d_wide),
        (out_n, 16, lanes),
    ):
        for stripe in range(width // lanes):
            here = pl.ds(at_row, height)
            total = kept[groups - 1, 3, here, :].astype(jnp.float32)
            for stage in range(groups - 1):
                total = total + from_far[stage, here, :].astype(jnp.float32)
            out[:, stripe * lanes : (stripe + 1) * lanes] = total
            at_row += height
    for stage in range(groups):
        for m in range(4):
            mate_copy(stage, m).wait_send()
        for m in range(2):
            one_copy(stage, m).wait_send()
        two_copy(stage).wait_send()
        if stage < groups - 1:
            far_copy(stage).wait_send()


def sum_gradients(groups, replicas, attn_in_t, d_qkv, ffn_in_t, d_gate_up, d_proj_t, mixed, d_down_t, act, gain_terms):
    tokens = d_qkv.shape[0]
    rows_in = D // groups
    thin = D // replicas
    q_part = d_qkv.shape[1] // replicas
    q_wide = -(-q_part // lanes) * lanes
    g_wide = d_gate_up.shape[1] // replicas
    o_wide = mixed.shape[1] // groups
    d_wide = act.shape[1] // groups
    d_qkv = jnp.pad(d_qkv.reshape(tokens, replicas, q_part), ((0, 0), (0, 0), (0, q_wide - q_part)))
    d_qkv = d_qkv.reshape(tokens, replicas * q_wide)
    share = gain_terms.shape[0] // (groups * replicas)
    gains = gain_terms.reshape(groups, replicas, 1, share).transpose(1, 0, 2, 3)
    gains = jnp.pad(gains, ((0, 0), (0, 0), (0, 15), (0, lanes - share))).astype(jnp.bfloat16)
    rows = (rows_in * (q_wide + g_wide) + thin * (o_wide + d_wide)) // lanes + 16
    dims = (rows_in, q_wide, g_wide, thin, o_wide, d_wide, rows)
    dma = pltpu.SemaphoreType.DMA
    vmem = pl.BlockSpec(memory_space=pltpu.VMEM)
    f32 = jnp.float32
    got = pl.pallas_call(
        functools.partial(sum_kernel, groups, replicas, dims),
        out_shape=[
            jax.ShapeDtypeStruct((rows_in, q_wide), f32),
            jax.ShapeDtypeStruct((rows_in, g_wide), f32),
            jax.ShapeDtypeStruct((thin, o_wide), f32),
            jax.ShapeDtypeStruct((thin, d_wide), f32),
            jax.ShapeDtypeStruct((16, lanes), f32),
        ],
        in_specs=[vmem] * 9,
        out_specs=[vmem] * 5,
        scratch_shapes=[
            pltpu.VMEM((groups, 4, rows, lanes), jnp.bfloat16),
            pltpu.VMEM((groups, 4, rows, lanes), jnp.bfloat16),
            pltpu.VMEM((groups, 4, rows, lanes), jnp.bfloat16),
            pltpu.VMEM((groups, 2, rows, lanes), jnp.bfloat16),
            pltpu.VMEM((groups, rows, lanes), jnp.bfloat16),
            pltpu.VMEM((groups - 1, rows, lanes), jnp.bfloat16),
            dma((groups, 4)), dma((groups, 4)),
            dma((groups, 2)), dma((groups, 2)),
            dma((groups,)), dma((groups,)),
            dma((groups - 1,)), dma((groups - 1,)),
        ],
        compiler_params=pltpu.CompilerParams(
            collective_id=2, has_side_effects=True, vmem_limit_bytes=48 * 1024 * 1024
        ),
        cost_estimate=pl.CostEstimate(flops=3000000000, bytes_accessed=12000000, transcendentals=0),
        name="sum_gradients",
    )(attn_in_t, d_qkv, ffn_in_t, d_gate_up, d_proj_t, mixed, d_down_t, act, gains)
    return (got[0][:, :q_part], got[2].T, got[1], got[3].T, got[4][0, :share])


def low(value):
    return value.astype(jnp.bfloat16)


def matmul(left, right):
    return jnp.dot(left, right, preferred_element_type=jnp.float32)


def rotate_norm(values, gain, cosine, sine):
    return rope_apply(norm_apply(values, gain), cosine, sine)


def before_kernel(hidden, w_qkv, gain_in, gain_q, gain_k, cosine, sine, attn_in_t, raw, query, keyval):
    attn_in = norm_apply(hidden[...].astype(jnp.float32), gain_in[...])
    attn_in_t[...] = low(attn_in.T)
    attn_in = low(attn_in)
    cos, sin = cosine[...], sine[...]
    for head in range(H + 2):
        here = slice(head * HD, (head + 1) * HD)
        part = matmul(attn_in, w_qkv[:, here])
        raw[:, here] = part
        if head < H:
            query[:, here] = low(rotate_norm(part, gain_q[...], cos, sin))
        elif head == H:
            keyval[:, :HD] = low(rotate_norm(part, gain_k[...], cos, sin))
        else:
            keyval[:, HD:] = low(part)


def middle_kernel(
    hidden, cotangent, query, keys, values, own_ids, key_ids, w_out, w_gate_up, w_down,
    gain_attn_out, gain_ffn_in, gain_ffn_out,
    block_out, mixed, ffn_in_t, act, d_down_t, d_gate_up, d_proj_t, d_query, d_keyval, d_residual,
    g_attn_out, g_ffn_in, g_ffn_out,
    bias, probs, gate_up, d_mixed, total,
):
    tokens = hidden.shape[0]
    span = keys.shape[0]
    scaling = HD ** (-0.5)
    row = lax.broadcasted_iota(jnp.int32, (tokens, span), 0) + (span - tokens)
    gap = row - lax.broadcasted_iota(jnp.int32, (tokens, span), 1)
    allowed = (own_ids[...] == key_ids[...]) & (gap >= 0) & (gap < WINDOW)
    bias[...] = jnp.where(allowed, 0.0, neg_fill)

    def head_columns(head):
        return pl.ds(pl.multiple_of(head * HD, HD), HD)

    def attend(head, carry):
        here = head_columns(head)
        scores = back_dot(query[:, here], keys[...]) * scaling + bias[...]
        expo = jnp.exp(scores - jnp.max(scores, axis=-1, keepdims=True))
        soft = expo * (1.0 / jnp.sum(expo, axis=-1, keepdims=True))
        probs[head] = soft
        mixed[:, here] = low(matmul(low(soft), values[...]))
        return carry

    lax.fori_loop(0, H, attend, 0)
    projected = matmul(mixed[...], w_out[...])
    residual = hidden[...].astype(jnp.float32) + norm_apply(projected, gain_attn_out[...])
    ffn_in = norm_apply(residual, gain_ffn_in[...])
    ffn_in_t[...] = low(ffn_in.T)
    ffn_low = low(ffn_in)
    part = 512

    def columns(i, base):
        return pl.ds(pl.multiple_of(base + i * part, part), part)

    total[...] = jnp.zeros_like(total)

    def forward(i, carry):
        gate = matmul(ffn_low, w_gate_up[:, columns(i, 0)])
        up = matmul(ffn_low, w_gate_up[:, columns(i, FF)])
        gate_up[:, columns(i, 0)] = gate
        gate_up[:, columns(i, FF)] = up
        product = low(gelu_product(gate, up))
        act[:, columns(i, 0)] = product
        total[...] += matmul(product, w_down[columns(i, 0), :])
        return carry

    lax.fori_loop(0, FF // part, forward, 0)
    upstream = cotangent[...].astype(jnp.float32)
    normed, pull = jax.vjp(norm_apply, total[...], gain_ffn_out[...])
    block_out[...] = low(residual + normed)
    d_down, g_ffn_out[...] = pull(upstream)
    d_down_t[...] = low(d_down.T)
    d_down_low = low(d_down)
    total[...] = jnp.zeros_like(total)

    def backward(i, carry):
        d_act = back_dot(d_down_low, w_down[columns(i, 0), :])
        unused, pull = jax.vjp(gelu_product, gate_up[:, columns(i, 0)], gate_up[:, columns(i, FF)])
        d_gate, d_up = pull(d_act)
        d_gate, d_up = low(d_gate), low(d_up)
        d_gate_up[:, columns(i, 0)] = d_gate
        d_gate_up[:, columns(i, FF)] = d_up
        total[...] += back_dot(d_gate, w_gate_up[:, columns(i, 0)]) + back_dot(
            d_up, w_gate_up[:, columns(i, FF)]
        )
        return carry

    lax.fori_loop(0, FF // part, backward, 0)
    unused, pull = jax.vjp(norm_apply, residual, gain_ffn_in[...])
    d_residual_ffn, g_ffn_in[...] = pull(total[...])
    d_res = upstream + d_residual_ffn
    d_residual[...] = d_res
    unused, pull = jax.vjp(norm_apply, projected, gain_attn_out[...])
    d_proj, g_attn_out[...] = pull(d_res)
    d_proj_t[...] = low(d_proj.T)
    d_mixed[...] = low(back_dot(low(d_proj), w_out[...]))
    d_keyval[...] = jnp.zeros_like(d_keyval)

    def attend_back(head, carry):
        here = head_columns(head)
        soft = probs[head]
        d_out = d_mixed[:, here]
        d_probs = back_dot(d_out, values[...])
        d_scores = low(soft * (d_probs - jnp.sum(d_probs * soft, axis=-1, keepdims=True)))
        d_query[:, here] = matmul(d_scores, keys[...]) * scaling
        d_keyval[:, :HD] += outer_sum(d_scores, query[:, here]) * scaling
        d_keyval[:, HD:] += outer_sum(low(soft), d_out)
        return carry

    lax.fori_loop(0, H, attend_back, 0)


def after_kernel(
    hidden, w_qkv, gain_in, gain_q, gain_k, cosine, sine, raw, d_query, d_own, d_residual,
    d_qkv, grad_in, g_in, g_q, g_k,
):
    cos, sin = cosine[...], sine[...]
    sums = None
    for head in range(H + 1):
        here = slice(head * HD, (head + 1) * HD)
        gain = gain_q if head < H else gain_k
        unused, pull = jax.vjp(lambda v, w: rotate_norm(v, w, cos, sin), raw[:, here], gain[...])
        d_raw, d_gain = pull(d_query[:, here] if head < H else d_own[:, :HD])
        d_qkv[:, here] = low(d_raw)
        if head < H:
            sums = d_gain if sums is None else sums + d_gain
        else:
            g_k[...] = d_gain
    g_q[...] = sums
    d_qkv[:, (H + 1) * HD :] = low(d_own[:, HD:])
    d_attn_in = back_dot(d_qkv[...], w_qkv[...])
    unused, pull = jax.vjp(norm_apply, hidden[...].astype(jnp.float32), gain_in[...])
    d_inputs, g_in[...] = pull(d_attn_in)
    grad_in[...] = low(d_residual[...] + d_inputs)


def plain_call(kernel, name, flops, outs, scratch, *args):
    vmem = pl.BlockSpec(memory_space=pltpu.VMEM)
    return pl.pallas_call(
        kernel,
        out_shape=[jax.ShapeDtypeStruct(shape, kind) for shape, kind in outs],
        in_specs=[vmem] * len(args),
        out_specs=[vmem] * len(outs),
        scratch_shapes=scratch,
        compiler_params=pltpu.CompilerParams(vmem_limit_bytes=56 * 1024 * 1024),
        cost_estimate=pl.CostEstimate(flops=flops, bytes_accessed=10000000, transcendentals=0),
        name=name,
    )(*args)


def layer_grads(
    hidden_in, cotangent, segment_ids, positions, full_qkv, full_out, full_gate_up, full_down, norm_gains
):
    tokens = hidden_in.shape[0]
    f32, b16 = jnp.float32, jnp.bfloat16
    gains = norm_gains[None, :]
    gain_attn_in, gain_attn_out, gain_ffn_in, gain_ffn_out = (
        gains[:, i * D : (i + 1) * D] for i in range(4)
    )
    gain_query = gains[:, 4 * D : 4 * D + HD]
    gain_key = gains[:, 4 * D + HD : 4 * D + 2 * HD]
    cosine, sine = rope_tables(positions, HD)
    wide = (H + 2) * HD
    attn_in_t, raw, query, keyval = plain_call(
        before_kernel, "before_attention", 2 * tokens * D * wide,
        [((D, tokens), b16), ((tokens, wide), f32), ((tokens, H * HD), b16), ((tokens, 2 * HD), b16)],
        [], hidden_in, full_qkv, gain_attn_in, gain_query, gain_key, cosine, sine,
    )
    reaches = -(-WINDOW // tokens)
    marks = jnp.broadcast_to((segment_ids + 1).astype(b16)[:, None], (tokens, lanes))
    moved = jnp.concatenate([keyval, marks], axis=1)
    parts = [moved]
    for reach in range(1, reaches + 1):
        parts.insert(0, shifted(moved, ("group", "replica"), reach))
    span = (reaches + 1) * tokens
    every = jnp.concatenate(parts, axis=0)
    key_ids = every[:, 2 * HD].astype(jnp.int32)[None, :]
    own_ids = (segment_ids + 1)[:, None]
    gain_out = ((1, D), f32)
    (
        block_out, mixed, ffn_in_t, act, d_down_t, d_gate_up, d_proj_t, d_query, d_keyval, d_residual,
        g_attn_out, g_ffn_in, g_ffn_out,
    ) = plain_call(
        middle_kernel, "attention_and_ffn", 8000000000,
        [
            ((tokens, D), b16), ((tokens, H * HD), b16), ((D, tokens), b16), ((tokens, FF), b16),
            ((D, tokens), b16), ((tokens, 2 * FF), b16), ((D, tokens), b16), ((tokens, H * HD), f32),
            ((span, 2 * HD), f32), ((tokens, D), f32), gain_out, gain_out, gain_out,
        ],
        [
            pltpu.VMEM((tokens, span), f32), pltpu.VMEM((H, tokens, span), f32),
            pltpu.VMEM((tokens, 2 * FF), f32), pltpu.VMEM((tokens, H * HD), b16),
            pltpu.VMEM((tokens, D), f32),
        ],
        hidden_in, cotangent, query, every[:, :HD], every[:, HD : 2 * HD], own_ids, key_ids,
        full_out, full_gate_up, full_down, gain_attn_out, gain_ffn_in, gain_ffn_out,
    )
    d_own = d_keyval[reaches * tokens :]
    for reach in range(1, reaches + 1):
        piece = d_keyval[(reaches - reach) * tokens : (reaches - reach + 1) * tokens]
        d_own = d_own + shifted(piece.astype(b16), ("group", "replica"), -reach).astype(f32)
    d_qkv, grad_in, g_in, g_q, g_k = plain_call(
        after_kernel, "after_attention", 2 * tokens * D * wide,
        [((tokens, wide), b16), ((tokens, D), b16), gain_out, ((1, HD), f32), ((1, HD), f32)],
        [], hidden_in, full_qkv, gain_attn_in, gain_query, gain_key, cosine, sine, raw, d_query, d_own,
        d_residual,
    )
    gain_terms = jnp.concatenate([g_in, g_attn_out, g_ffn_in, g_ffn_out, g_q, g_k], axis=1)[0]
    return block_out, grad_in, (
        attn_in_t, d_qkv, ffn_in_t, d_gate_up, d_proj_t, mixed, d_down_t, act, gain_terms
    )


def owned_sums(groups, replicas, terms):
    attn_in_t, d_qkv, ffn_in_t, d_gate_up, d_proj_t, mixed, d_down_t, act, gain_terms = terms
    column = lax.axis_index("replica")
    gain_rows = gain_terms.reshape(groups, gain_terms.shape[0] // groups)
    terms = (
        matmul(attn_in_t, d_qkv),
        outer_sum(mixed, d_proj_t.T),
        matmul(ffn_in_t, d_gate_up),
        outer_sum(act, d_down_t.T),
        gain_rows,
    )
    row_sums = (
        lax.psum_scatter(
            terms[0].astype(jnp.bfloat16), "group", scatter_dimension=0, tiled=True
        ).astype(jnp.float32),
        lax.psum_scatter(
            terms[1].astype(jnp.bfloat16), "group", scatter_dimension=0, tiled=True
        ).astype(jnp.float32),
        lax.psum_scatter(
            terms[2].astype(jnp.bfloat16), "group", scatter_dimension=0, tiled=True
        ).astype(jnp.float32),
        lax.psum_scatter(
            terms[3].astype(jnp.bfloat16), "group", scatter_dimension=0, tiled=True
        ).astype(jnp.float32),
        lax.psum_scatter(
            terms[4].astype(jnp.bfloat16), "group", scatter_dimension=0, tiled=True
        ).astype(jnp.float32),
    )
    totals = lax.psum((row_sums[0], row_sums[1], row_sums[2], row_sums[3], row_sums[4]), "replica")
    owned = tuple(
        (
            lax.dynamic_slice_in_dim(
                item, column * (item.shape[1] // replicas), item.shape[1] // replicas, 1
            )
            for item in totals
        )
    )
    return owned[:4] + (owned[4].reshape(-1),)


def body(
    hidden_in,
    cotangent,
    segment_ids,
    positions,
    w_qkv,
    w_out,
    w_gate_up,
    w_down,
    norm_gains,
    first_qkv,
    first_out,
    first_gate_up,
    first_down,
    first_gains,
    second_qkv,
    second_out,
    second_gate_up,
    second_down,
    second_gains,
):
    groups = lax.axis_size("group")
    replicas = lax.axis_size("replica")
    direct = (groups, replicas) == (4, 8)
    if direct:
        full_qkv, full_out, full_gate_up, full_down = gather_weights(
            groups, replicas, w_qkv, w_out, w_gate_up, w_down
        )
    else:
        full_qkv, full_out, full_gate_up, full_down = (
            lax.all_gather(w_qkv, "group", axis=0, tiled=True),
            lax.all_gather(w_out, "group", axis=0, tiled=True),
            lax.all_gather(w_gate_up, "group", axis=0, tiled=True),
            lax.all_gather(w_down, "group", axis=0, tiled=True),
        )
    block_out, grad_in, terms = layer_grads(
        hidden_in, cotangent, segment_ids, positions, full_qkv, full_out, full_gate_up, full_down, norm_gains
    )
    if direct:
        owned = sum_gradients(groups, replicas, *terms)
    else:
        owned = owned_sums(groups, replicas, terms)
    column = lax.axis_index("replica")

    def old_columns(weight):
        width = weight.shape[1] // replicas
        return lax.dynamic_slice_in_dim(weight, column * width, width, 1).astype(jnp.float32)

    moment_qkv, new_qkv = adam_step(
        owned[0], first_qkv, second_qkv, old_columns(w_qkv), weight_decay
    )
    moment_out, new_out = adam_step(
        owned[1], first_out, second_out, old_columns(w_out), weight_decay
    )
    moment_gate_up, new_gate_up = adam_step(
        owned[2], first_gate_up, second_gate_up, old_columns(w_gate_up), weight_decay
    )
    moment_down, new_down = adam_step(
        owned[3], first_down, second_down, old_columns(w_down), weight_decay
    )
    grad_gains = owned[4]
    share = grad_gains.shape[0]
    owner = lax.axis_index("group") * replicas + column
    old_gains = lax.dynamic_slice_in_dim(norm_gains, owner * share, share, 0)
    moment_gains, new_gains = adam_step(grad_gains, first_gains, second_gains, old_gains, 0.0)
    return (
        block_out,
        grad_in,
        owned[0],
        owned[1],
        owned[2],
        owned[3],
        grad_gains,
        moment_qkv,
        moment_out,
        moment_gate_up,
        moment_down,
        moment_gains,
        new_qkv,
        new_out,
        new_gate_up,
        new_down,
        new_gains,
    )


def solution(mesh):
    in_specs = (
        P(("group", "replica"), None),
        P(("group", "replica"), None),
        P(("group", "replica")),
        P(("group", "replica")),
        P("group", None),
        P("group", None),
        P("group", None),
        P("group", None),
        P(),
        P("group", "replica"),
        P("group", "replica"),
        P("group", "replica"),
        P("group", "replica"),
        P(("group", "replica")),
        P("group", "replica"),
        P("group", "replica"),
        P("group", "replica"),
        P("group", "replica"),
        P(("group", "replica")),
    )
    out_specs = (
        P(("group", "replica"), None),
        P(("group", "replica"), None),
        P("group", "replica"),
        P("group", "replica"),
        P("group", "replica"),
        P("group", "replica"),
        P(("group", "replica")),
        P("group", "replica"),
        P("group", "replica"),
        P("group", "replica"),
        P("group", "replica"),
        P(("group", "replica")),
        P("group", "replica"),
        P("group", "replica"),
        P("group", "replica"),
        P("group", "replica"),
        P(("group", "replica")),
    )
    return jax.shard_map(body, mesh=mesh, in_specs=in_specs, out_specs=out_specs, check_vma=False)
```

```python
import functools

import jax
import jax.numpy as jnp
from jax import lax
from jax.experimental import pallas as pl
from jax.experimental.pallas import tpu as pltpu
from jax.sharding import PartitionSpec as P

MESH = pl.DeviceIdType.MESH

D = 640
H = 4
HD = 256
FF = 2048
WINDOW = 512
STEP = 10


norm_epsilon = 1e-06
rope_base = 10000.0
beta_one = 0.9
beta_two = 0.999
adam_epsilon = 1e-08
learn_rate = 0.05
weight_decay = 0.1
neg_fill = -1e30


def shifted(value, axis, by):
    peers = lax.axis_size(axis)
    pairs = [(i, i + by) for i in range(peers) if 0 <= i + by < peers]
    return lax.ppermute(value, axis, pairs)


def norm_apply(values, gain):
    scale = lax.rsqrt(jnp.mean(values * values, axis=-1, keepdims=True) + norm_epsilon)
    return values * scale * (1.0 + gain)


def rope_tables(positions, width):
    freqs = rope_base ** (-jnp.arange(0, width, 2).astype(jnp.float32) / width)
    angles = positions.astype(jnp.float32)[:, None] * freqs[None, :]
    return (jnp.cos(angles), jnp.sin(angles))


def rope_apply(values, cosine, sine):
    half = values.shape[-1] // 2
    first = values[..., :half]
    second = values[..., half:]
    return jnp.concatenate(
        [first * cosine - second * sine, second * cosine + first * sine], axis=-1
    )


def gelu_product(gate, up):
    return jax.nn.gelu(gate, approximate=True) * up


def outer_sum(left, right):
    return lax.dot_general(
        left, right, (((0,), (0,)), ((), ())), preferred_element_type=jnp.float32
    )


def back_dot(grad, weight):
    return lax.dot_general(
        grad, weight, (((1,), (1,)), ((), ())), preferred_element_type=jnp.float32
    )


def adam_step(grad, first, second, old, decay):
    first_new = beta_one * first + (1.0 - beta_one) * grad
    second_new = beta_two * second + (1.0 - beta_two) * grad * grad
    first_hat = first_new / (1.0 - beta_one**STEP)
    second_hat = second_new / (1.0 - beta_two**STEP)
    new = old - learn_rate * (first_hat / (jnp.sqrt(second_hat) + adam_epsilon) + decay * old)
    return (second_new, new)


def places():
    g = lax.axis_index("group")
    r = lax.axis_index("replica")
    core = lax.rem(r, 2)
    x = lax.rem(r // 2, 2)
    y = r // 4
    mate = r + 1 - 2 * core
    over_x = 2 - 4 * x
    over_y = 4 - 8 * y
    step_one = over_x * (1 - core) + over_y * core
    step_two = over_y * (1 - core) + over_x * core
    return g, r, mate, step_one, step_two


def meet(g, r, mate, one, two, groups):
    barrier = pltpu.get_barrier_semaphore()
    for to in (mate, one, two):
        pl.semaphore_signal(barrier, inc=1, device_id=(g, to), device_id_type=MESH)
    for far in range(1, groups):
        to = lax.rem(g + far, groups)
        pl.semaphore_signal(barrier, inc=1, device_id=(to, r), device_id_type=MESH)
    pl.semaphore_wait(barrier, 2 + groups)


def gather_kernel(groups, replicas, *refs):
    shards, fulls = refs[:4], refs[4:8]
    local_sem, a_send, a_recv, b_send, b_recv = refs[8:]
    g, r, mate, step_one, step_two = places()
    one, two = r + step_one, r + step_two
    diagonal = r + step_one + step_two
    chips = replicas // 2

    def view(ref, which, height, base, index):
        width = ref.shape[1]
        if which == 0:
            rows = height // 2
            part = width // chips
            return ref.at[
                pl.ds(pl.multiple_of(base + lax.rem(index, 2) * rows, 16), rows),
                pl.ds(pl.multiple_of((index // 2) * part, 128), part),
            ]
        if which == 2:
            part = width // replicas
            return ref.at[
                pl.ds(pl.multiple_of(base, 16), height),
                pl.ds(pl.multiple_of(index * part, 128), part),
            ]
        rows = height // replicas
        return ref.at[pl.ds(pl.multiple_of(base + index * rows, 16), rows), :]

    def place(which, group, index):
        height = shards[which].shape[0]
        return view(fulls[which], which, height, group * height, index)

    def send(src, dst, send_sem, recv_sem, to):
        return pltpu.make_async_remote_copy(
            src_ref=src, dst_ref=dst, send_sem=send_sem, recv_sem=recv_sem,
            device_id=to, device_id_type=MESH,
        )

    meet(g, r, mate, one, two, groups)
    started = []
    items = [(which, far) for which in range(4) for far in range(1, groups)]
    for which, far in items:
        shard = shards[which]
        copy = send(
            view(shard, which, shard.shape[0], 0, r),
            place(which, g, r),
            a_send.at[far - 1, which],
            a_recv.at[far - 1, which],
            (lax.rem(g + far, groups), r),
        )
        copy.start()
        started.append(copy)
    own = []
    for which in range(4):
        height = shards[which].shape[0]
        copy = pltpu.make_async_copy(
            shards[which],
            fulls[which].at[pl.ds(pl.multiple_of(g * height, 16), height), :],
            local_sem.at[which],
        )
        copy.start()
        own.append(copy)

    def push(item, slot, index, to):
        which, far = items[item]
        part = place(which, lax.rem(g + groups - far, groups), index)
        copy = send(part, part, b_send.at[item, slot], b_recv.at[item, slot], (g, to))
        copy.start()
        started.append(copy)

    def arrived(item, slot, index):
        which, far = items[item]
        part = place(which, lax.rem(g + groups - far, groups), index)
        send(part, part, b_send.at[item, slot], b_recv.at[item, slot], (g, mate)).wait_recv()

    for turn in range(len(items) + 5):
        if turn < len(items):
            which, far = items[turn]
            part = place(which, lax.rem(g + groups - far, groups), r)
            send(
                part, part, a_send.at[far - 1, which], a_recv.at[far - 1, which], (g, mate)
            ).wait_recv()
            push(turn, 0, r, one)
            push(turn, 1, r, two)
            push(turn, 3, r, mate)
        item = turn - 2
        if 0 <= item < len(items):
            arrived(item, 0, one)
            push(item, 2, one, two)
            push(item, 4, one, mate)
        item = turn - 5
        if 0 <= item < len(items):
            arrived(item, 1, two)
            push(item, 5, two, mate)
            arrived(item, 2, diagonal)
            push(item, 6, diagonal, mate)
    for item in range(len(items)):
        arrived(item, 3, mate)
        arrived(item, 4, mate + step_two)
        arrived(item, 5, mate + step_one)
        arrived(item, 6, mate + step_one + step_two)
    for copy in own:
        copy.wait()
    for copy in started:
        copy.wait_send()


def gather_weights(groups, replicas, *shards):
    items = 4 * (groups - 1)
    dma = pltpu.SemaphoreType.DMA
    return pl.pallas_call(
        functools.partial(gather_kernel, groups, replicas),
        out_shape=[
            jax.ShapeDtypeStruct((groups * s.shape[0], s.shape[1]), s.dtype) for s in shards
        ],
        in_specs=[pl.BlockSpec(memory_space=pltpu.VMEM)] * 4,
        out_specs=[pl.BlockSpec(memory_space=pltpu.VMEM)] * 4,
        scratch_shapes=[
            dma((4,)),
            dma((groups - 1, 4)),
            dma((groups - 1, 4)),
            dma((items, 7)),
            dma((items, 7)),
        ],
        compiler_params=pltpu.CompilerParams(
            collective_id=1, has_side_effects=True, vmem_limit_bytes=48 * 1024 * 1024
        ),
        cost_estimate=pl.CostEstimate(flops=0, bytes_accessed=25000000, transcendentals=0),
        name="gather_weights",
    )(*shards)


lanes = 128


def sum_kernel(groups, replicas, dims, *refs):
    (at, dqkv, bt, dgu, dzt, o, dmt, f, gains) = refs[:9]
    out_q, out_g, out_o, out_d, out_n = refs[9:14]
    to_mate, kept, from_mate, from_one, from_two, from_far = refs[14:20]
    c_send, c_recv, x_send, x_recv, y_send, y_recv, z_send, z_recv = refs[20:]
    rows_in, q_wide, g_wide, thin, o_wide, d_wide, rows = dims
    g, r, mate, step_one, step_two = places()
    one, two = r + step_one, r + step_two

    def dot(left, right):
        return jnp.dot(left, right, preferred_element_type=jnp.float32).astype(jnp.bfloat16)

    def compute(dst, group, index):
        top = pl.ds(pl.multiple_of(group * rows_in, 16), rows_in)
        side = pl.ds(pl.multiple_of(index * thin, 16), thin)

        def columns(width, place):
            return pl.ds(pl.multiple_of(place * width, 128), width)

        at_row = 0
        for left, right, height, width in (
            (at[top, :], dqkv[:, columns(q_wide, index)], rows_in, q_wide),
            (bt[top, :], dgu[:, columns(g_wide, index)], rows_in, g_wide),
            (dzt[side, :], o[:, columns(o_wide, group)], thin, o_wide),
            (dmt[side, :], f[:, columns(d_wide, group)], thin, d_wide),
        ):
            block = dot(left, right)
            for stripe in range(width // lanes):
                dst[pl.ds(at_row, height), :] = block[:, stripe * lanes : (stripe + 1) * lanes]
                at_row += height
        dst[pl.ds(at_row, 16), :] = gains[index, group]

    def send(src, dst, send_sem, recv_sem, to):
        return pltpu.make_async_remote_copy(
            src_ref=src, dst_ref=dst, send_sem=send_sem, recv_sem=recv_sem,
            device_id=to, device_id_type=MESH,
        )

    def add(dst, src):
        part = 208
        def body(i, carry):
            here = pl.ds(pl.multiple_of(i * part, 16), part)
            dst[here, :] = (
                dst[here, :].astype(jnp.float32) + src[here, :].astype(jnp.float32)
            ).astype(jnp.bfloat16)
            return carry
        lax.fori_loop(0, rows // part, body, 0)

    def flips(m):
        return 1 - m // 2, lax.rem((m + 1) // 2, 2)

    def target(stage):
        return lax.rem(g + 1 + stage, groups)

    def mate_copy(stage, m):
        return send(
            to_mate.at[stage, m], from_mate.at[stage, m], c_send.at[stage, m], c_recv.at[stage, m],
            (g, mate),
        )

    def one_copy(stage, m):
        return send(
            kept.at[stage, m], from_one.at[stage, 1 - m], x_send.at[stage, 1 - m],
            x_recv.at[stage, 1 - m], (g, one),
        )

    def two_copy(stage):
        return send(
            kept.at[stage, 2], from_two.at[stage], y_send.at[stage], y_recv.at[stage], (g, two)
        )

    def far_copy(stage):
        return send(
            kept.at[stage, 3], from_far.at[stage], z_send.at[stage], z_recv.at[stage],
            (target(stage), r),
        )

    def make(stage):
        def for_mate(m, carry):
            first, second = flips(m)
            compute(
                to_mate.at[stage, m], target(stage), mate + first * step_two + second * step_one
            )
            mate_copy(stage, m).start()
            return carry

        def for_me(m, carry):
            first, second = flips(m)
            compute(kept.at[stage, m], target(stage), r + first * step_one + second * step_two)
            return carry

        lax.fori_loop(0, 4, for_mate, 0)
        lax.fori_loop(0, 4, for_me, 0)

    def pass_one(stage):
        for m in (1, 0):
            mate_copy(stage, m).wait_recv()
            add(kept.at[stage, m], from_mate.at[stage, m])
            one_copy(stage, m).start()
        for m in (2, 3):
            mate_copy(stage, m).wait_recv()
            add(kept.at[stage, m], from_mate.at[stage, m])

    def pass_two(stage):
        one_copy(stage, 1).wait_recv()
        add(kept.at[stage, 2], from_one.at[stage, 0])
        two_copy(stage).start()
        one_copy(stage, 0).wait_recv()
        add(kept.at[stage, 3], from_one.at[stage, 1])

    def pass_far(stage):
        two_copy(stage).wait_recv()
        add(kept.at[stage, 3], from_two.at[stage])
        if stage < groups - 1:
            far_copy(stage).start()

    meet(g, r, mate, one, two, groups)
    for turn in range(groups + 2):
        if turn < groups:
            make(turn)
            pass_one(turn)
        if 0 <= turn - 1 < groups:
            pass_two(turn - 1)
        if 0 <= turn - 2 < groups:
            pass_far(turn - 2)
    for stage in range(groups - 1):
        far_copy(stage).wait_recv()
    at_row = 0
    for out, height, width in (
        (out_q, rows_in, q_wide),
        (out_g, rows_in, g_wide),
        (out_o, thin, o_wide),
        (out_d, thin, d_wide),
        (out_n, 16, lanes),
    ):
        for stripe in range(width // lanes):
            here = pl.ds(at_row, height)
            total = kept[groups - 1, 3, here, :].astype(jnp.float32)
            for stage in range(groups - 1):
                total = total + from_far[stage, here, :].astype(jnp.float32)
            out[:, stripe * lanes : (stripe + 1) * lanes] = total
            at_row += height
    for stage in range(groups):
        for m in range(4):
            mate_copy(stage, m).wait_send()
        for m in range(2):
            one_copy(stage, m).wait_send()
        two_copy(stage).wait_send()
        if stage < groups - 1:
            far_copy(stage).wait_send()


def sum_gradients(groups, replicas, attn_in_t, d_qkv, ffn_in_t, d_gate_up, d_proj_t, mixed, d_down_t, act, gain_terms):
    tokens = d_qkv.shape[0]
    rows_in = D // groups
    thin = D // replicas
    q_part = d_qkv.shape[1] // replicas
    q_wide = -(-q_part // lanes) * lanes
    g_wide = d_gate_up.shape[1] // replicas
    o_wide = mixed.shape[1] // groups
    d_wide = act.shape[1] // groups
    d_qkv = jnp.pad(d_qkv.reshape(tokens, replicas, q_part), ((0, 0), (0, 0), (0, q_wide - q_part)))
    d_qkv = d_qkv.reshape(tokens, replicas * q_wide)
    share = gain_terms.shape[0] // (groups * replicas)
    gains = gain_terms.reshape(groups, replicas, 1, share).transpose(1, 0, 2, 3)
    gains = jnp.pad(gains, ((0, 0), (0, 0), (0, 15), (0, lanes - share))).astype(jnp.bfloat16)
    rows = (rows_in * (q_wide + g_wide) + thin * (o_wide + d_wide)) // lanes + 16
    dims = (rows_in, q_wide, g_wide, thin, o_wide, d_wide, rows)
    dma = pltpu.SemaphoreType.DMA
    vmem = pl.BlockSpec(memory_space=pltpu.VMEM)
    f32 = jnp.float32
    got = pl.pallas_call(
        functools.partial(sum_kernel, groups, replicas, dims),
        out_shape=[
            jax.ShapeDtypeStruct((rows_in, q_wide), f32),
            jax.ShapeDtypeStruct((rows_in, g_wide), f32),
            jax.ShapeDtypeStruct((thin, o_wide), f32),
            jax.ShapeDtypeStruct((thin, d_wide), f32),
            jax.ShapeDtypeStruct((16, lanes), f32),
        ],
        in_specs=[vmem] * 9,
        out_specs=[vmem] * 5,
        scratch_shapes=[
            pltpu.VMEM((groups, 4, rows, lanes), jnp.bfloat16),
            pltpu.VMEM((groups, 4, rows, lanes), jnp.bfloat16),
            pltpu.VMEM((groups, 4, rows, lanes), jnp.bfloat16),
            pltpu.VMEM((groups, 2, rows, lanes), jnp.bfloat16),
            pltpu.VMEM((groups, rows, lanes), jnp.bfloat16),
            pltpu.VMEM((groups - 1, rows, lanes), jnp.bfloat16),
            dma((groups, 4)), dma((groups, 4)),
            dma((groups, 2)), dma((groups, 2)),
            dma((groups,)), dma((groups,)),
            dma((groups - 1,)), dma((groups - 1,)),
        ],
        compiler_params=pltpu.CompilerParams(
            collective_id=2, has_side_effects=True, vmem_limit_bytes=48 * 1024 * 1024
        ),
        cost_estimate=pl.CostEstimate(flops=3000000000, bytes_accessed=12000000, transcendentals=0),
        name="sum_gradients",
    )(attn_in_t, d_qkv, ffn_in_t, d_gate_up, d_proj_t, mixed, d_down_t, act, gains)
    return (got[0][:, :q_part], got[2].T, got[1], got[3].T, got[4][0, :share])


def low(value):
    return value.astype(jnp.bfloat16)


def matmul(left, right):
    return jnp.dot(left, right, preferred_element_type=jnp.float32)


def rotate_norm(values, gain, cosine, sine):
    return rope_apply(norm_apply(values, gain), cosine, sine)


def before_kernel(
    hidden, w_qkv, gain_in, gain_q, gain_k, cosine, sine, ids, attn_in_t, raw, query, keyval
):
    marks = (ids[...] + 1).astype(jnp.float32)
    keyval[:, 2 * HD :] = low(jnp.broadcast_to(marks, (marks.shape[0], lanes)))
    attn_in = norm_apply(hidden[...].astype(jnp.float32), gain_in[...])
    attn_in_t[...] = low(attn_in.T)
    attn_in = low(attn_in)
    cos, sin = cosine[...], sine[...]
    for head in range(H + 2):
        here = slice(head * HD, (head + 1) * HD)
        part = matmul(attn_in, w_qkv[:, here])
        raw[:, here] = part
        if head < H:
            query[:, here] = low(rotate_norm(part, gain_q[...], cos, sin))
        elif head == H:
            keyval[:, :HD] = low(rotate_norm(part, gain_k[...], cos, sin))
        else:
            keyval[:, HD : 2 * HD] = low(part)


def middle_kernel(reaches, *refs):
    parts, refs = refs[: reaches + 1], refs[reaches + 1 :]
    (hidden, cotangent, query, w_out, w_gate_up, w_down, gain_attn_out, gain_ffn_in, gain_ffn_out) = refs[:9]
    d_parts, refs = refs[9 : 10 + reaches], refs[10 + reaches :]
    (
        block_out, mixed, ffn_in_t, act, d_down_t, d_gate_up, d_proj_t, d_query, d_residual,
        g_attn_out, g_ffn_in, g_ffn_out,
        bias, probs, gate_up, d_mixed, total, keys, values, d_keyval,
    ) = refs
    tokens = hidden.shape[0]
    span = keys.shape[0]
    marks = []
    for at, part in enumerate(parts):
        here = slice(at * tokens, (at + 1) * tokens)
        keys[here, :] = part[:, :HD]
        values[here, :] = part[:, HD : 2 * HD]
        marks.append(part[:, 2 * HD :].astype(jnp.float32))
    key_ids = jnp.concatenate([mark.T[:1, :] for mark in marks], axis=1)
    own_ids = marks[-1][:, :1]
    scaling = HD ** (-0.5)
    row = lax.broadcasted_iota(jnp.int32, (tokens, span), 0) + (span - tokens)
    gap = row - lax.broadcasted_iota(jnp.int32, (tokens, span), 1)
    allowed = (own_ids == key_ids) & (gap >= 0) & (gap < WINDOW)
    bias[...] = jnp.where(allowed, 0.0, neg_fill)

    def head_columns(head):
        return pl.ds(pl.multiple_of(head * HD, HD), HD)

    def attend(head, carry):
        here = head_columns(head)
        scores = back_dot(query[:, here], keys[...]) * scaling + bias[...]
        expo = jnp.exp(scores - jnp.max(scores, axis=-1, keepdims=True))
        soft = expo * (1.0 / jnp.sum(expo, axis=-1, keepdims=True))
        probs[head] = soft
        mixed[:, here] = low(matmul(low(soft), values[...]))
        return carry

    lax.fori_loop(0, H, attend, 0)
    projected = matmul(mixed[...], w_out[...])
    residual = hidden[...].astype(jnp.float32) + norm_apply(projected, gain_attn_out[...])
    ffn_in = norm_apply(residual, gain_ffn_in[...])
    ffn_in_t[...] = low(ffn_in.T)
    ffn_low = low(ffn_in)
    part = 512

    def columns(i, base):
        return pl.ds(pl.multiple_of(base + i * part, part), part)

    total[...] = jnp.zeros_like(total)

    def forward(i, carry):
        gate = matmul(ffn_low, w_gate_up[:, columns(i, 0)])
        up = matmul(ffn_low, w_gate_up[:, columns(i, FF)])
        gate_up[:, columns(i, 0)] = gate
        gate_up[:, columns(i, FF)] = up
        product = low(gelu_product(gate, up))
        act[:, columns(i, 0)] = product
        total[...] += matmul(product, w_down[columns(i, 0), :])
        return carry

    lax.fori_loop(0, FF // part, forward, 0)
    upstream = cotangent[...].astype(jnp.float32)
    normed, pull = jax.vjp(norm_apply, total[...], gain_ffn_out[...])
    block_out[...] = low(residual + normed)
    d_down, g_ffn_out[...] = pull(upstream)
    d_down_t[...] = low(d_down.T)
    d_down_low = low(d_down)
    total[...] = jnp.zeros_like(total)

    def backward(i, carry):
        d_act = back_dot(d_down_low, w_down[columns(i, 0), :])
        unused, pull = jax.vjp(gelu_product, gate_up[:, columns(i, 0)], gate_up[:, columns(i, FF)])
        d_gate, d_up = pull(d_act)
        d_gate, d_up = low(d_gate), low(d_up)
        d_gate_up[:, columns(i, 0)] = d_gate
        d_gate_up[:, columns(i, FF)] = d_up
        total[...] += back_dot(d_gate, w_gate_up[:, columns(i, 0)]) + back_dot(
            d_up, w_gate_up[:, columns(i, FF)]
        )
        return carry

    lax.fori_loop(0, FF // part, backward, 0)
    unused, pull = jax.vjp(norm_apply, residual, gain_ffn_in[...])
    d_residual_ffn, g_ffn_in[...] = pull(total[...])
    d_res = upstream + d_residual_ffn
    d_residual[...] = d_res
    unused, pull = jax.vjp(norm_apply, projected, gain_attn_out[...])
    d_proj, g_attn_out[...] = pull(d_res)
    d_proj_t[...] = low(d_proj.T)
    d_mixed[...] = low(back_dot(low(d_proj), w_out[...]))
    d_keyval[...] = jnp.zeros_like(d_keyval)

    def attend_back(head, carry):
        here = head_columns(head)
        soft = probs[head]
        d_out = d_mixed[:, here]
        d_probs = back_dot(d_out, values[...])
        d_scores = low(soft * (d_probs - jnp.sum(d_probs * soft, axis=-1, keepdims=True)))
        d_query[:, here] = matmul(d_scores, keys[...]) * scaling
        d_keyval[:, :HD] += outer_sum(d_scores, query[:, here]) * scaling
        d_keyval[:, HD:] += outer_sum(low(soft), d_out)
        return carry

    lax.fori_loop(0, H, attend_back, 0)
    for at, part in enumerate(d_parts):
        part[...] = d_keyval[at * tokens : (at + 1) * tokens, :].astype(part.dtype)


def after_query_kernel(w_query, gain_q, cosine, sine, raw, d_query, d_low, d_attn_in, g_q):
    cos, sin = cosine[...], sine[...]
    sums = None
    for head in range(H):
        here = slice(head * HD, (head + 1) * HD)
        unused, pull = jax.vjp(lambda v, w: rotate_norm(v, w, cos, sin), raw[:, here], gain_q[...])
        d_raw, d_gain = pull(d_query[:, here])
        d_low[:, here] = low(d_raw)
        sums = d_gain if sums is None else sums + d_gain
    g_q[...] = sums
    d_attn_in[...] = back_dot(d_low[...], w_query[:, : H * HD])


def after_key_kernel(reaches, *refs):
    came, refs = refs[:reaches], refs[reaches:]
    (
        hidden, w_qkv, gain_in, gain_k, cosine, sine, raw, d_own, d_query_low, d_attn_query, d_residual,
        d_qkv, grad_in, g_in, g_k,
    ) = refs
    d_keyval = d_own[...]
    for part in came:
        d_keyval = d_keyval + part[...].astype(jnp.float32)
    cos, sin = cosine[...], sine[...]
    at_key = slice(H * HD, (H + 1) * HD)
    unused, pull = jax.vjp(lambda v, w: rotate_norm(v, w, cos, sin), raw[:, at_key], gain_k[...])
    d_raw, g_k[...] = pull(d_keyval[:, :HD])
    d_qkv[:, : H * HD] = d_query_low[...]
    d_qkv[:, at_key] = low(d_raw)
    d_qkv[:, (H + 1) * HD :] = low(d_keyval[:, HD:])
    d_attn_in = d_attn_query[...] + back_dot(d_qkv[:, H * HD :], w_qkv[:, H * HD :])
    unused, pull = jax.vjp(norm_apply, hidden[...].astype(jnp.float32), gain_in[...])
    d_inputs, g_in[...] = pull(d_attn_in)
    grad_in[...] = low(d_residual[...] + d_inputs)


def plain_call(kernel, name, flops, outs, scratch, *args):
    vmem = pl.BlockSpec(memory_space=pltpu.VMEM)
    return pl.pallas_call(
        kernel,
        out_shape=[jax.ShapeDtypeStruct(shape, kind) for shape, kind in outs],
        in_specs=[vmem] * len(args),
        out_specs=[vmem] * len(outs),
        scratch_shapes=scratch,
        compiler_params=pltpu.CompilerParams(vmem_limit_bytes=56 * 1024 * 1024),
        cost_estimate=pl.CostEstimate(flops=flops, bytes_accessed=10000000, transcendentals=0),
        name=name,
    )(*args)


def layer_grads(
    hidden_in, cotangent, segment_ids, positions, full_qkv, full_out, full_gate_up, full_down, norm_gains
):
    tokens = hidden_in.shape[0]
    f32, b16 = jnp.float32, jnp.bfloat16
    gains = norm_gains[None, :]
    gain_attn_in, gain_attn_out, gain_ffn_in, gain_ffn_out = (
        gains[:, i * D : (i + 1) * D] for i in range(4)
    )
    gain_query = gains[:, 4 * D : 4 * D + HD]
    gain_key = gains[:, 4 * D + HD : 4 * D + 2 * HD]
    cosine, sine = rope_tables(positions, HD)
    wide = (H + 2) * HD
    attn_in_t, raw, query, moved = plain_call(
        before_kernel, "before_attention", 2 * tokens * D * wide,
        [((D, tokens), b16), ((tokens, wide), f32), ((tokens, H * HD), b16), ((tokens, 2 * HD + lanes), b16)],
        [], hidden_in, full_qkv, gain_attn_in, gain_query, gain_key, cosine, sine, segment_ids[:, None],
    )
    reaches = -(-WINDOW // tokens)
    parts = [moved]
    for reach in range(1, reaches + 1):
        parts.insert(0, shifted(moved, ("group", "replica"), reach))
    span = (reaches + 1) * tokens
    gain_out = ((1, D), f32)
    done = plain_call(
        functools.partial(middle_kernel, reaches), "attention_and_ffn", 8000000000,
        [((tokens, 2 * HD), b16)] * reaches + [
            ((tokens, 2 * HD), f32),
            ((tokens, D), b16), ((tokens, H * HD), b16), ((D, tokens), b16), ((tokens, FF), b16),
            ((D, tokens), b16), ((tokens, 2 * FF), b16), ((D, tokens), b16), ((tokens, H * HD), f32),
            ((tokens, D), f32), gain_out, gain_out, gain_out,
        ],
        [
            pltpu.VMEM((tokens, span), f32), pltpu.VMEM((H, tokens, span), f32),
            pltpu.VMEM((tokens, 2 * FF), f32), pltpu.VMEM((tokens, H * HD), b16),
            pltpu.VMEM((tokens, D), f32), pltpu.VMEM((span, HD), b16), pltpu.VMEM((span, HD), b16),
            pltpu.VMEM((span, 2 * HD), f32),
        ],
        *parts, hidden_in, cotangent, query,
        full_out, full_gate_up, full_down, gain_attn_out, gain_ffn_in, gain_ffn_out,
    )
    d_parts, d_own = done[:reaches], done[reaches]
    (
        block_out, mixed, ffn_in_t, act, d_down_t, d_gate_up, d_proj_t, d_query, d_residual,
        g_attn_out, g_ffn_in, g_ffn_out,
    ) = done[reaches + 1 :]
    came = [
        shifted(d_parts[reaches - reach], ("group", "replica"), -reach)
        for reach in range(1, reaches + 1)
    ]
    d_query_low, d_attn_query, g_q = plain_call(
        after_query_kernel, "after_attention_query", 2 * tokens * D * H * HD,
        [((tokens, H * HD), b16), ((tokens, D), f32), ((1, HD), f32)],
        [], full_qkv, gain_query, cosine, sine, raw, d_query,
    )
    d_qkv, grad_in, g_in, g_k = plain_call(
        functools.partial(after_key_kernel, reaches), "after_attention_key", 2 * tokens * D * 2 * HD,
        [((tokens, wide), b16), ((tokens, D), b16), gain_out, ((1, HD), f32)],
        [], *came, hidden_in, full_qkv, gain_attn_in, gain_key, cosine, sine, raw, d_own, d_query_low,
        d_attn_query, d_residual,
    )
    gain_terms = jnp.concatenate([g_in, g_attn_out, g_ffn_in, g_ffn_out, g_q, g_k], axis=1)[0]
    return block_out, grad_in, (
        attn_in_t, d_qkv, ffn_in_t, d_gate_up, d_proj_t, mixed, d_down_t, act, gain_terms
    )


def owned_sums(groups, replicas, terms):
    attn_in_t, d_qkv, ffn_in_t, d_gate_up, d_proj_t, mixed, d_down_t, act, gain_terms = terms
    column = lax.axis_index("replica")
    gain_rows = gain_terms.reshape(groups, gain_terms.shape[0] // groups)
    terms = (
        matmul(attn_in_t, d_qkv),
        outer_sum(mixed, d_proj_t.T),
        matmul(ffn_in_t, d_gate_up),
        outer_sum(act, d_down_t.T),
        gain_rows,
    )
    row_sums = (
        lax.psum_scatter(
            terms[0].astype(jnp.bfloat16), "group", scatter_dimension=0, tiled=True
        ).astype(jnp.float32),
        lax.psum_scatter(
            terms[1].astype(jnp.bfloat16), "group", scatter_dimension=0, tiled=True
        ).astype(jnp.float32),
        lax.psum_scatter(
            terms[2].astype(jnp.bfloat16), "group", scatter_dimension=0, tiled=True
        ).astype(jnp.float32),
        lax.psum_scatter(
            terms[3].astype(jnp.bfloat16), "group", scatter_dimension=0, tiled=True
        ).astype(jnp.float32),
        lax.psum_scatter(
            terms[4].astype(jnp.bfloat16), "group", scatter_dimension=0, tiled=True
        ).astype(jnp.float32),
    )
    totals = lax.psum((row_sums[0], row_sums[1], row_sums[2], row_sums[3], row_sums[4]), "replica")
    owned = tuple(
        (
            lax.dynamic_slice_in_dim(
                item, column * (item.shape[1] // replicas), item.shape[1] // replicas, 1
            )
            for item in totals
        )
    )
    return owned[:4] + (owned[4].reshape(-1),)


def body(
    hidden_in,
    cotangent,
    segment_ids,
    positions,
    w_qkv,
    w_out,
    w_gate_up,
    w_down,
    norm_gains,
    first_qkv,
    first_out,
    first_gate_up,
    first_down,
    first_gains,
    second_qkv,
    second_out,
    second_gate_up,
    second_down,
    second_gains,
):
    groups = lax.axis_size("group")
    replicas = lax.axis_size("replica")
    direct = (groups, replicas) == (4, 8)
    if direct:
        full_qkv, full_out, full_gate_up, full_down = gather_weights(
            groups, replicas, w_qkv, w_out, w_gate_up, w_down
        )
    else:
        full_qkv, full_out, full_gate_up, full_down = (
            lax.all_gather(w_qkv, "group", axis=0, tiled=True),
            lax.all_gather(w_out, "group", axis=0, tiled=True),
            lax.all_gather(w_gate_up, "group", axis=0, tiled=True),
            lax.all_gather(w_down, "group", axis=0, tiled=True),
        )
    block_out, grad_in, terms = layer_grads(
        hidden_in, cotangent, segment_ids, positions, full_qkv, full_out, full_gate_up, full_down, norm_gains
    )
    if direct:
        owned = sum_gradients(groups, replicas, *terms)
    else:
        owned = owned_sums(groups, replicas, terms)
    column = lax.axis_index("replica")

    def old_columns(weight):
        width = weight.shape[1] // replicas
        return lax.dynamic_slice_in_dim(weight, column * width, width, 1).astype(jnp.float32)

    moment_qkv, new_qkv = adam_step(
        owned[0], first_qkv, second_qkv, old_columns(w_qkv), weight_decay
    )
    moment_out, new_out = adam_step(
        owned[1], first_out, second_out, old_columns(w_out), weight_decay
    )
    moment_gate_up, new_gate_up = adam_step(
        owned[2], first_gate_up, second_gate_up, old_columns(w_gate_up), weight_decay
    )
    moment_down, new_down = adam_step(
        owned[3], first_down, second_down, old_columns(w_down), weight_decay
    )
    grad_gains = owned[4]
    share = grad_gains.shape[0]
    owner = lax.axis_index("group") * replicas + column
    old_gains = lax.dynamic_slice_in_dim(norm_gains, owner * share, share, 0)
    moment_gains, new_gains = adam_step(grad_gains, first_gains, second_gains, old_gains, 0.0)
    return (
        block_out,
        grad_in,
        owned[0],
        owned[1],
        owned[2],
        owned[3],
        grad_gains,
        moment_qkv,
        moment_out,
        moment_gate_up,
        moment_down,
        moment_gains,
        new_qkv,
        new_out,
        new_gate_up,
        new_down,
        new_gains,
    )


def solution(mesh):
    in_specs = (
        P(("group", "replica"), None),
        P(("group", "replica"), None),
        P(("group", "replica")),
        P(("group", "replica")),
        P("group", None),
        P("group", None),
        P("group", None),
        P("group", None),
        P(),
        P("group", "replica"),
        P("group", "replica"),
        P("group", "replica"),
        P("group", "replica"),
        P(("group", "replica")),
        P("group", "replica"),
        P("group", "replica"),
        P("group", "replica"),
        P("group", "replica"),
        P(("group", "replica")),
    )
    out_specs = (
        P(("group", "replica"), None),
        P(("group", "replica"), None),
        P("group", "replica"),
        P("group", "replica"),
        P("group", "replica"),
        P("group", "replica"),
        P(("group", "replica")),
        P("group", "replica"),
        P("group", "replica"),
        P("group", "replica"),
        P("group", "replica"),
        P(("group", "replica")),
        P("group", "replica"),
        P("group", "replica"),
        P("group", "replica"),
        P("group", "replica"),
        P(("group", "replica")),
    )
    return jax.shard_map(body, mesh=mesh, in_specs=in_specs, out_specs=out_specs, check_vma=False)
```

```python
import functools

import jax
import jax.numpy as jnp
from jax import lax
from jax.experimental import pallas as pl
from jax.experimental.pallas import tpu as pltpu
from jax.sharding import PartitionSpec as P

MESH = pl.DeviceIdType.MESH

D = 640
H = 4
HD = 256
FF = 2048
WINDOW = 512
STEP = 10


norm_epsilon = 1e-06
rope_base = 10000.0
beta_one = 0.9
beta_two = 0.999
adam_epsilon = 1e-08
learn_rate = 0.05
weight_decay = 0.1
neg_fill = -1e30


def shifted(value, axis, by):
    peers = lax.axis_size(axis)
    pairs = [(i, i + by) for i in range(peers) if 0 <= i + by < peers]
    return lax.ppermute(value, axis, pairs)


def norm_apply(values, gain):
    scale = lax.rsqrt(jnp.mean(values * values, axis=-1, keepdims=True) + norm_epsilon)
    return values * scale * (1.0 + gain)


def rope_tables(positions, width):
    freqs = rope_base ** (-jnp.arange(0, width, 2).astype(jnp.float32) / width)
    angles = positions.astype(jnp.float32)[:, None] * freqs[None, :]
    return (jnp.cos(angles), jnp.sin(angles))


def rope_apply(values, cosine, sine):
    half = values.shape[-1] // 2
    first = values[..., :half]
    second = values[..., half:]
    return jnp.concatenate(
        [first * cosine - second * sine, second * cosine + first * sine], axis=-1
    )


def gelu_product(gate, up):
    return jax.nn.gelu(gate, approximate=True) * up


def outer_sum(left, right):
    return lax.dot_general(
        left, right, (((0,), (0,)), ((), ())), preferred_element_type=jnp.float32
    )


def back_dot(grad, weight):
    return lax.dot_general(
        grad, weight, (((1,), (1,)), ((), ())), preferred_element_type=jnp.float32
    )


def adam_step(grad, first, second, old, decay):
    first_new = beta_one * first + (1.0 - beta_one) * grad
    second_new = beta_two * second + (1.0 - beta_two) * grad * grad
    first_hat = first_new / (1.0 - beta_one**STEP)
    second_hat = second_new / (1.0 - beta_two**STEP)
    new = old - learn_rate * (first_hat / (jnp.sqrt(second_hat) + adam_epsilon) + decay * old)
    return (second_new, new)


def places():
    g = lax.axis_index("group")
    r = lax.axis_index("replica")
    core = lax.rem(r, 2)
    x = lax.rem(r // 2, 2)
    y = r // 4
    mate = r + 1 - 2 * core
    over_x = 2 - 4 * x
    over_y = 4 - 8 * y
    step_one = over_x * (1 - core) + over_y * core
    step_two = over_y * (1 - core) + over_x * core
    return g, r, mate, step_one, step_two


def meet(g, r, mate, one, two, groups):
    barrier = pltpu.get_barrier_semaphore()
    for to in (mate, one, two):
        pl.semaphore_signal(barrier, inc=1, device_id=(g, to), device_id_type=MESH)
    for far in range(1, groups):
        to = lax.rem(g + far, groups)
        pl.semaphore_signal(barrier, inc=1, device_id=(to, r), device_id_type=MESH)
    pl.semaphore_wait(barrier, 2 + groups)


def gather_kernel(groups, replicas, *refs):
    shards, fulls = refs[:4], refs[4:8]
    local_sem, a_send, a_recv, b_send, b_recv = refs[8:]
    g, r, mate, step_one, step_two = places()
    one, two = r + step_one, r + step_two
    diagonal = r + step_one + step_two
    chips = replicas // 2

    def view(ref, which, height, base, index):
        width = ref.shape[1]
        if which == 0:
            rows = height // 2
            part = width // chips
            return ref.at[
                pl.ds(pl.multiple_of(base + lax.rem(index, 2) * rows, 16), rows),
                pl.ds(pl.multiple_of((index // 2) * part, 128), part),
            ]
        if which == 2:
            part = width // replicas
            return ref.at[
                pl.ds(pl.multiple_of(base, 16), height),
                pl.ds(pl.multiple_of(index * part, 128), part),
            ]
        rows = height // replicas
        return ref.at[pl.ds(pl.multiple_of(base + index * rows, 16), rows), :]

    def place(which, group, index):
        height = shards[which].shape[0]
        return view(fulls[which], which, height, group * height, index)

    def send(src, dst, send_sem, recv_sem, to):
        return pltpu.make_async_remote_copy(
            src_ref=src, dst_ref=dst, send_sem=send_sem, recv_sem=recv_sem,
            device_id=to, device_id_type=MESH,
        )

    meet(g, r, mate, one, two, groups)
    started = []
    items = [(which, far) for which in range(4) for far in range(1, groups)]
    for which, far in items:
        shard = shards[which]
        copy = send(
            view(shard, which, shard.shape[0], 0, r),
            place(which, g, r),
            a_send.at[far - 1, which],
            a_recv.at[far - 1, which],
            (lax.rem(g + far, groups), r),
        )
        copy.start()
        started.append(copy)
    own = []
    for which in range(4):
        height = shards[which].shape[0]
        copy = pltpu.make_async_copy(
            shards[which],
            fulls[which].at[pl.ds(pl.multiple_of(g * height, 16), height), :],
            local_sem.at[which],
        )
        copy.start()
        own.append(copy)

    def push(item, slot, index, to):
        which, far = items[item]
        part = place(which, lax.rem(g + groups - far, groups), index)
        copy = send(part, part, b_send.at[item, slot], b_recv.at[item, slot], (g, to))
        copy.start()
        started.append(copy)

    def arrived(item, slot, index):
        which, far = items[item]
        part = place(which, lax.rem(g + groups - far, groups), index)
        send(part, part, b_send.at[item, slot], b_recv.at[item, slot], (g, mate)).wait_recv()

    for turn in range(len(items) + 5):
        if turn < len(items):
            which, far = items[turn]
            part = place(which, lax.rem(g + groups - far, groups), r)
            send(
                part, part, a_send.at[far - 1, which], a_recv.at[far - 1, which], (g, mate)
            ).wait_recv()
            push(turn, 0, r, one)
            push(turn, 1, r, two)
            push(turn, 3, r, mate)
        item = turn - 2
        if 0 <= item < len(items):
            arrived(item, 0, one)
            push(item, 2, one, two)
            push(item, 4, one, mate)
        item = turn - 5
        if 0 <= item < len(items):
            arrived(item, 1, two)
            push(item, 5, two, mate)
            arrived(item, 2, diagonal)
            push(item, 6, diagonal, mate)
    for item in range(len(items)):
        arrived(item, 3, mate)
        arrived(item, 4, mate + step_two)
        arrived(item, 5, mate + step_one)
        arrived(item, 6, mate + step_one + step_two)
    for copy in own:
        copy.wait()
    for copy in started:
        copy.wait_send()


def gather_weights(groups, replicas, *shards):
    items = 4 * (groups - 1)
    dma = pltpu.SemaphoreType.DMA
    return pl.pallas_call(
        functools.partial(gather_kernel, groups, replicas),
        out_shape=[
            jax.ShapeDtypeStruct((groups * s.shape[0], s.shape[1]), s.dtype) for s in shards
        ],
        in_specs=[pl.BlockSpec(memory_space=pltpu.VMEM)] * 4,
        out_specs=[pl.BlockSpec(memory_space=pltpu.VMEM)] * 4,
        scratch_shapes=[
            dma((4,)),
            dma((groups - 1, 4)),
            dma((groups - 1, 4)),
            dma((items, 7)),
            dma((items, 7)),
        ],
        compiler_params=pltpu.CompilerParams(
            collective_id=1, has_side_effects=True, vmem_limit_bytes=48 * 1024 * 1024
        ),
        cost_estimate=pl.CostEstimate(flops=0, bytes_accessed=25000000, transcendentals=0),
        name="gather_weights",
    )(*shards)


lanes = 128


def sum_kernel(groups, replicas, dims, *refs):
    (at, dqkv, bt, dgu, dzt, o, dmt, f, gains) = refs[:9]
    out_q, out_g, out_o, out_d, out_n = refs[9:14]
    to_mate, kept, from_mate, from_one, from_two, from_far = refs[14:20]
    c_send, c_recv, x_send, x_recv, y_send, y_recv, z_send, z_recv = refs[20:]
    rows_in, q_wide, g_wide, thin, o_wide, d_wide, rows = dims
    g, r, mate, step_one, step_two = places()
    one, two = r + step_one, r + step_two

    def dot(left, right):
        return jnp.dot(left, right, preferred_element_type=jnp.float32).astype(jnp.bfloat16)

    def compute(dst, group, index):
        top = pl.ds(pl.multiple_of(group * rows_in, 16), rows_in)
        side = pl.ds(pl.multiple_of(index * thin, 16), thin)

        def columns(width, place):
            return pl.ds(pl.multiple_of(place * width, 128), width)

        at_row = 0
        for left, right, height, width in (
            (at[top, :], dqkv[:, columns(q_wide, index)], rows_in, q_wide),
            (bt[top, :], dgu[:, columns(g_wide, index)], rows_in, g_wide),
            (dzt[side, :], o[:, columns(o_wide, group)], thin, o_wide),
            (dmt[side, :], f[:, columns(d_wide, group)], thin, d_wide),
        ):
            block = dot(left, right)
            for stripe in range(width // lanes):
                dst[pl.ds(at_row, height), :] = block[:, stripe * lanes : (stripe + 1) * lanes]
                at_row += height
        dst[pl.ds(at_row, 16), :] = gains[index, group]

    def send(src, dst, send_sem, recv_sem, to):
        return pltpu.make_async_remote_copy(
            src_ref=src, dst_ref=dst, send_sem=send_sem, recv_sem=recv_sem,
            device_id=to, device_id_type=MESH,
        )

    def add(dst, src):
        part = 208
        def body(i, carry):
            here = pl.ds(pl.multiple_of(i * part, 16), part)
            dst[here, :] = (
                dst[here, :].astype(jnp.float32) + src[here, :].astype(jnp.float32)
            ).astype(jnp.bfloat16)
            return carry
        lax.fori_loop(0, rows // part, body, 0)

    def flips(m):
        return 1 - m // 2, lax.rem((m + 1) // 2, 2)

    def target(stage):
        return lax.rem(g + 1 + stage, groups)

    def mate_copy(stage, m):
        return send(
            to_mate.at[stage, m], from_mate.at[stage, m], c_send.at[stage, m], c_recv.at[stage, m],
            (g, mate),
        )

    def one_copy(stage, m):
        return send(
            kept.at[stage, m], from_one.at[stage, 1 - m], x_send.at[stage, 1 - m],
            x_recv.at[stage, 1 - m], (g, one),
        )

    def two_copy(stage):
        return send(
            kept.at[stage, 2], from_two.at[stage], y_send.at[stage], y_recv.at[stage], (g, two)
        )

    def far_copy(stage):
        return send(
            kept.at[stage, 3], from_far.at[stage], z_send.at[stage], z_recv.at[stage],
            (target(stage), r),
        )

    def make(stage):
        def for_mate(m, carry):
            first, second = flips(m)
            compute(
                to_mate.at[stage, m], target(stage), mate + first * step_two + second * step_one
            )
            mate_copy(stage, m).start()
            return carry

        def for_me(m, carry):
            first, second = flips(m)
            compute(kept.at[stage, m], target(stage), r + first * step_one + second * step_two)
            return carry

        lax.fori_loop(0, 4, for_mate, 0)
        lax.fori_loop(0, 2, for_me, 0)
        pass_one(stage)
        lax.fori_loop(2, 4, for_me, 0)

    def pass_one(stage):
        for m in (1, 0):
            mate_copy(stage, m).wait_recv()
            add(kept.at[stage, m], from_mate.at[stage, m])
            one_copy(stage, m).start()

    def pass_rest(stage):
        for m in (2, 3):
            mate_copy(stage, m).wait_recv()
            add(kept.at[stage, m], from_mate.at[stage, m])

    def pass_two(stage):
        one_copy(stage, 1).wait_recv()
        add(kept.at[stage, 2], from_one.at[stage, 0])
        two_copy(stage).start()
        one_copy(stage, 0).wait_recv()
        add(kept.at[stage, 3], from_one.at[stage, 1])

    def pass_far(stage):
        two_copy(stage).wait_recv()
        add(kept.at[stage, 3], from_two.at[stage])
        if stage < groups - 1:
            far_copy(stage).start()

    meet(g, r, mate, one, two, groups)
    for turn in range(groups + 2):
        if turn < groups:
            make(turn)
            pass_rest(turn)
        if 0 <= turn - 1 < groups:
            pass_two(turn - 1)
        if 0 <= turn - 2 < groups:
            pass_far(turn - 2)
    for stage in range(groups - 1):
        far_copy(stage).wait_recv()
    at_row = 0
    for out, height, width in (
        (out_q, rows_in, q_wide),
        (out_g, rows_in, g_wide),
        (out_o, thin, o_wide),
        (out_d, thin, d_wide),
        (out_n, 16, lanes),
    ):
        for stripe in range(width // lanes):
            here = pl.ds(at_row, height)
            total = kept[groups - 1, 3, here, :].astype(jnp.float32)
            for stage in range(groups - 1):
                total = total + from_far[stage, here, :].astype(jnp.float32)
            out[:, stripe * lanes : (stripe + 1) * lanes] = total
            at_row += height
    for stage in range(groups):
        for m in range(4):
            mate_copy(stage, m).wait_send()
        for m in range(2):
            one_copy(stage, m).wait_send()
        two_copy(stage).wait_send()
        if stage < groups - 1:
            far_copy(stage).wait_send()


def sum_gradients(groups, replicas, attn_in_t, d_qkv, ffn_in_t, d_gate_up, d_proj_t, mixed, d_down_t, act, gain_terms):
    tokens = d_qkv.shape[0]
    rows_in = D // groups
    thin = D // replicas
    q_part = d_qkv.shape[1] // replicas
    q_wide = -(-q_part // lanes) * lanes
    g_wide = d_gate_up.shape[1] // replicas
    o_wide = mixed.shape[1] // groups
    d_wide = act.shape[1] // groups
    d_qkv = jnp.pad(d_qkv.reshape(tokens, replicas, q_part), ((0, 0), (0, 0), (0, q_wide - q_part)))
    d_qkv = d_qkv.reshape(tokens, replicas * q_wide)
    share = gain_terms.shape[0] // (groups * replicas)
    gains = gain_terms.reshape(groups, replicas, 1, share).transpose(1, 0, 2, 3)
    gains = jnp.pad(gains, ((0, 0), (0, 0), (0, 15), (0, lanes - share))).astype(jnp.bfloat16)
    rows = (rows_in * (q_wide + g_wide) + thin * (o_wide + d_wide)) // lanes + 16
    dims = (rows_in, q_wide, g_wide, thin, o_wide, d_wide, rows)
    dma = pltpu.SemaphoreType.DMA
    vmem = pl.BlockSpec(memory_space=pltpu.VMEM)
    f32 = jnp.float32
    got = pl.pallas_call(
        functools.partial(sum_kernel, groups, replicas, dims),
        out_shape=[
            jax.ShapeDtypeStruct((rows_in, q_wide), f32),
            jax.ShapeDtypeStruct((rows_in, g_wide), f32),
            jax.ShapeDtypeStruct((thin, o_wide), f32),
            jax.ShapeDtypeStruct((thin, d_wide), f32),
            jax.ShapeDtypeStruct((16, lanes), f32),
        ],
        in_specs=[vmem] * 9,
        out_specs=[vmem] * 5,
        scratch_shapes=[
            pltpu.VMEM((groups, 4, rows, lanes), jnp.bfloat16),
            pltpu.VMEM((groups, 4, rows, lanes), jnp.bfloat16),
            pltpu.VMEM((groups, 4, rows, lanes), jnp.bfloat16),
            pltpu.VMEM((groups, 2, rows, lanes), jnp.bfloat16),
            pltpu.VMEM((groups, rows, lanes), jnp.bfloat16),
            pltpu.VMEM((groups - 1, rows, lanes), jnp.bfloat16),
            dma((groups, 4)), dma((groups, 4)),
            dma((groups, 2)), dma((groups, 2)),
            dma((groups,)), dma((groups,)),
            dma((groups - 1,)), dma((groups - 1,)),
        ],
        compiler_params=pltpu.CompilerParams(
            collective_id=2, has_side_effects=True, vmem_limit_bytes=48 * 1024 * 1024
        ),
        cost_estimate=pl.CostEstimate(flops=3000000000, bytes_accessed=12000000, transcendentals=0),
        name="sum_gradients",
    )(attn_in_t, d_qkv, ffn_in_t, d_gate_up, d_proj_t, mixed, d_down_t, act, gains)
    return (got[0][:, :q_part], got[2].T, got[1], got[3].T, got[4][0, :share])


def low(value):
    return value.astype(jnp.bfloat16)


def matmul(left, right):
    return jnp.dot(left, right, preferred_element_type=jnp.float32)


def rotate_norm(values, gain, cosine, sine):
    return rope_apply(norm_apply(values, gain), cosine, sine)


def before_kernel(
    hidden, w_qkv, gain_in, gain_q, gain_k, cosine, sine, ids, attn_in_t, raw, query, keyval
):
    marks = (ids[...] + 1).astype(jnp.float32)
    keyval[:, 2 * HD :] = low(jnp.broadcast_to(marks, (marks.shape[0], lanes)))
    attn_in = norm_apply(hidden[...].astype(jnp.float32), gain_in[...])
    attn_in_t[...] = low(attn_in.T)
    attn_in = low(attn_in)
    cos, sin = cosine[...], sine[...]
    for head in range(H + 2):
        here = slice(head * HD, (head + 1) * HD)
        part = matmul(attn_in, w_qkv[:, here])
        raw[:, here] = part
        if head < H:
            query[:, here] = low(rotate_norm(part, gain_q[...], cos, sin))
        elif head == H:
            keyval[:, :HD] = low(rotate_norm(part, gain_k[...], cos, sin))
        else:
            keyval[:, HD : 2 * HD] = low(part)


def middle_kernel(reaches, *refs):
    parts, refs = refs[: reaches + 1], refs[reaches + 1 :]
    (hidden, cotangent, query, w_out, w_gate_up, w_down, gain_attn_out, gain_ffn_in, gain_ffn_out) = refs[:9]
    d_parts, refs = refs[9 : 10 + reaches], refs[10 + reaches :]
    (
        block_out, mixed, ffn_in_t, act, d_down_t, d_gate_up, d_proj_t, d_query, d_residual,
        g_attn_out, g_ffn_in, g_ffn_out,
        bias, probs, gate_up, d_mixed, total, keys, values, d_keyval,
    ) = refs
    tokens = hidden.shape[0]
    span = keys.shape[0]
    marks = []
    for at, part in enumerate(parts):
        here = slice(at * tokens, (at + 1) * tokens)
        keys[here, :] = part[:, :HD]
        values[here, :] = part[:, HD : 2 * HD]
        marks.append(part[:, 2 * HD :].astype(jnp.float32))
    key_ids = jnp.concatenate([mark.T[:1, :] for mark in marks], axis=1)
    own_ids = marks[-1][:, :1]
    scaling = HD ** (-0.5)
    row = lax.broadcasted_iota(jnp.int32, (tokens, span), 0) + (span - tokens)
    gap = row - lax.broadcasted_iota(jnp.int32, (tokens, span), 1)
    allowed = (own_ids == key_ids) & (gap >= 0) & (gap < WINDOW)
    bias[...] = jnp.where(allowed, 0.0, neg_fill)

    def head_columns(head):
        return pl.ds(pl.multiple_of(head * HD, HD), HD)

    def attend(head, carry):
        here = head_columns(head)
        scores = back_dot(query[:, here], keys[...]) * scaling + bias[...]
        expo = jnp.exp(scores - jnp.max(scores, axis=-1, keepdims=True))
        soft = expo * (1.0 / jnp.sum(expo, axis=-1, keepdims=True))
        probs[head] = soft
        mixed[:, here] = low(matmul(low(soft), values[...]))
        return carry

    lax.fori_loop(0, H, attend, 0)
    projected = matmul(mixed[...], w_out[...])
    residual = hidden[...].astype(jnp.float32) + norm_apply(projected, gain_attn_out[...])
    ffn_in = norm_apply(residual, gain_ffn_in[...])
    ffn_in_t[...] = low(ffn_in.T)
    ffn_low = low(ffn_in)
    part = 512

    def columns(i, base):
        return pl.ds(pl.multiple_of(base + i * part, part), part)

    total[...] = jnp.zeros_like(total)

    def forward(i, carry):
        gate = matmul(ffn_low, w_gate_up[:, columns(i, 0)])
        up = matmul(ffn_low, w_gate_up[:, columns(i, FF)])
        gate_up[:, columns(i, 0)] = gate
        gate_up[:, columns(i, FF)] = up
        product = low(gelu_product(gate, up))
        act[:, columns(i, 0)] = product
        total[...] += matmul(product, w_down[columns(i, 0), :])
        return carry

    lax.fori_loop(0, FF // part, forward, 0)
    upstream = cotangent[...].astype(jnp.float32)
    normed, pull = jax.vjp(norm_apply, total[...], gain_ffn_out[...])
    block_out[...] = low(residual + normed)
    d_down, g_ffn_out[...] = pull(upstream)
    d_down_t[...] = low(d_down.T)
    d_down_low = low(d_down)
    total[...] = jnp.zeros_like(total)

    def backward(i, carry):
        d_act = back_dot(d_down_low, w_down[columns(i, 0), :])
        unused, pull = jax.vjp(gelu_product, gate_up[:, columns(i, 0)], gate_up[:, columns(i, FF)])
        d_gate, d_up = pull(d_act)
        d_gate, d_up = low(d_gate), low(d_up)
        d_gate_up[:, columns(i, 0)] = d_gate
        d_gate_up[:, columns(i, FF)] = d_up
        total[...] += back_dot(d_gate, w_gate_up[:, columns(i, 0)]) + back_dot(
            d_up, w_gate_up[:, columns(i, FF)]
        )
        return carry

    lax.fori_loop(0, FF // part, backward, 0)
    unused, pull = jax.vjp(norm_apply, residual, gain_ffn_in[...])
    d_residual_ffn, g_ffn_in[...] = pull(total[...])
    d_res = upstream + d_residual_ffn
    d_residual[...] = d_res
    unused, pull = jax.vjp(norm_apply, projected, gain_attn_out[...])
    d_proj, g_attn_out[...] = pull(d_res)
    d_proj_t[...] = low(d_proj.T)
    d_mixed[...] = low(back_dot(low(d_proj), w_out[...]))
    d_keyval[...] = jnp.zeros_like(d_keyval)

    def attend_back(head, carry):
        here = head_columns(head)
        soft = probs[head]
        d_out = d_mixed[:, here]
        d_probs = back_dot(d_out, values[...])
        d_scores = low(soft * (d_probs - jnp.sum(d_probs * soft, axis=-1, keepdims=True)))
        d_query[:, here] = matmul(d_scores, keys[...]) * scaling
        d_keyval[:, :HD] += outer_sum(d_scores, query[:, here]) * scaling
        d_keyval[:, HD:] += outer_sum(low(soft), d_out)
        return carry

    lax.fori_loop(0, H, attend_back, 0)
    for at, part in enumerate(d_parts):
        part[...] = d_keyval[at * tokens : (at + 1) * tokens, :].astype(part.dtype)


def after_query_kernel(w_query, gain_q, cosine, sine, raw, d_query, d_low, d_attn_in, g_q):
    cos, sin = cosine[...], sine[...]
    sums = None
    for head in range(H):
        here = slice(head * HD, (head + 1) * HD)
        unused, pull = jax.vjp(lambda v, w: rotate_norm(v, w, cos, sin), raw[:, here], gain_q[...])
        d_raw, d_gain = pull(d_query[:, here])
        d_low[:, here] = low(d_raw)
        sums = d_gain if sums is None else sums + d_gain
    g_q[...] = sums
    d_attn_in[...] = back_dot(d_low[...], w_query[:, : H * HD])


def after_key_kernel(reaches, *refs):
    came, refs = refs[:reaches], refs[reaches:]
    (
        hidden, w_qkv, gain_in, gain_k, cosine, sine, raw, d_own, d_query_low, d_attn_query, d_residual,
        d_qkv, grad_in, g_in, g_k,
    ) = refs
    d_keyval = d_own[...]
    for part in came:
        d_keyval = d_keyval + part[...].astype(jnp.float32)
    cos, sin = cosine[...], sine[...]
    at_key = slice(H * HD, (H + 1) * HD)
    unused, pull = jax.vjp(lambda v, w: rotate_norm(v, w, cos, sin), raw[:, at_key], gain_k[...])
    d_raw, g_k[...] = pull(d_keyval[:, :HD])
    d_qkv[:, : H * HD] = d_query_low[...]
    d_qkv[:, at_key] = low(d_raw)
    d_qkv[:, (H + 1) * HD :] = low(d_keyval[:, HD:])
    d_attn_in = d_attn_query[...] + back_dot(d_qkv[:, H * HD :], w_qkv[:, H * HD :])
    unused, pull = jax.vjp(norm_apply, hidden[...].astype(jnp.float32), gain_in[...])
    d_inputs, g_in[...] = pull(d_attn_in)
    grad_in[...] = low(d_residual[...] + d_inputs)


def plain_call(kernel, name, flops, outs, scratch, *args):
    vmem = pl.BlockSpec(memory_space=pltpu.VMEM)
    return pl.pallas_call(
        kernel,
        out_shape=[jax.ShapeDtypeStruct(shape, kind) for shape, kind in outs],
        in_specs=[vmem] * len(args),
        out_specs=[vmem] * len(outs),
        scratch_shapes=scratch,
        compiler_params=pltpu.CompilerParams(vmem_limit_bytes=56 * 1024 * 1024),
        cost_estimate=pl.CostEstimate(flops=flops, bytes_accessed=10000000, transcendentals=0),
        name=name,
    )(*args)


def layer_grads(
    hidden_in, cotangent, segment_ids, positions, full_qkv, full_out, full_gate_up, full_down, norm_gains
):
    tokens = hidden_in.shape[0]
    f32, b16 = jnp.float32, jnp.bfloat16
    gains = norm_gains[None, :]
    gain_attn_in, gain_attn_out, gain_ffn_in, gain_ffn_out = (
        gains[:, i * D : (i + 1) * D] for i in range(4)
    )
    gain_query = gains[:, 4 * D : 4 * D + HD]
    gain_key = gains[:, 4 * D + HD : 4 * D + 2 * HD]
    cosine, sine = rope_tables(positions, HD)
    wide = (H + 2) * HD
    attn_in_t, raw, query, moved = plain_call(
        before_kernel, "before_attention", 2 * tokens * D * wide,
        [((D, tokens), b16), ((tokens, wide), f32), ((tokens, H * HD), b16), ((tokens, 2 * HD + lanes), b16)],
        [], hidden_in, full_qkv, gain_attn_in, gain_query, gain_key, cosine, sine, segment_ids[:, None],
    )
    reaches = -(-WINDOW // tokens)
    parts = [moved]
    for reach in range(1, reaches + 1):
        parts.insert(0, shifted(moved, ("group", "replica"), reach))
    span = (reaches + 1) * tokens
    gain_out = ((1, D), f32)
    done = plain_call(
        functools.partial(middle_kernel, reaches), "attention_and_ffn", 8000000000,
        [((tokens, 2 * HD), b16)] * reaches + [
            ((tokens, 2 * HD), f32),
            ((tokens, D), b16), ((tokens, H * HD), b16), ((D, tokens), b16), ((tokens, FF), b16),
            ((D, tokens), b16), ((tokens, 2 * FF), b16), ((D, tokens), b16), ((tokens, H * HD), f32),
            ((tokens, D), f32), gain_out, gain_out, gain_out,
        ],
        [
            pltpu.VMEM((tokens, span), f32), pltpu.VMEM((H, tokens, span), f32),
            pltpu.VMEM((tokens, 2 * FF), f32), pltpu.VMEM((tokens, H * HD), b16),
            pltpu.VMEM((tokens, D), f32), pltpu.VMEM((span, HD), b16), pltpu.VMEM((span, HD), b16),
            pltpu.VMEM((span, 2 * HD), f32),
        ],
        *parts, hidden_in, cotangent, query,
        full_out, full_gate_up, full_down, gain_attn_out, gain_ffn_in, gain_ffn_out,
    )
    d_parts, d_own = done[:reaches], done[reaches]
    (
        block_out, mixed, ffn_in_t, act, d_down_t, d_gate_up, d_proj_t, d_query, d_residual,
        g_attn_out, g_ffn_in, g_ffn_out,
    ) = done[reaches + 1 :]
    came = [
        shifted(d_parts[reaches - reach], ("group", "replica"), -reach)
        for reach in range(1, reaches + 1)
    ]
    d_query_low, d_attn_query, g_q = plain_call(
        after_query_kernel, "after_attention_query", 2 * tokens * D * H * HD,
        [((tokens, H * HD), b16), ((tokens, D), f32), ((1, HD), f32)],
        [], full_qkv, gain_query, cosine, sine, raw, d_query,
    )
    d_qkv, grad_in, g_in, g_k = plain_call(
        functools.partial(after_key_kernel, reaches), "after_attention_key", 2 * tokens * D * 2 * HD,
        [((tokens, wide), b16), ((tokens, D), b16), gain_out, ((1, HD), f32)],
        [], *came, hidden_in, full_qkv, gain_attn_in, gain_key, cosine, sine, raw, d_own, d_query_low,
        d_attn_query, d_residual,
    )
    gain_terms = jnp.concatenate([g_in, g_attn_out, g_ffn_in, g_ffn_out, g_q, g_k], axis=1)[0]
    return block_out, grad_in, (
        attn_in_t, d_qkv, ffn_in_t, d_gate_up, d_proj_t, mixed, d_down_t, act, gain_terms
    )


def owned_sums(groups, replicas, terms):
    attn_in_t, d_qkv, ffn_in_t, d_gate_up, d_proj_t, mixed, d_down_t, act, gain_terms = terms
    column = lax.axis_index("replica")
    gain_rows = gain_terms.reshape(groups, gain_terms.shape[0] // groups)
    terms = (
        matmul(attn_in_t, d_qkv),
        outer_sum(mixed, d_proj_t.T),
        matmul(ffn_in_t, d_gate_up),
        outer_sum(act, d_down_t.T),
        gain_rows,
    )
    row_sums = (
        lax.psum_scatter(
            terms[0].astype(jnp.bfloat16), "group", scatter_dimension=0, tiled=True
        ).astype(jnp.float32),
        lax.psum_scatter(
            terms[1].astype(jnp.bfloat16), "group", scatter_dimension=0, tiled=True
        ).astype(jnp.float32),
        lax.psum_scatter(
            terms[2].astype(jnp.bfloat16), "group", scatter_dimension=0, tiled=True
        ).astype(jnp.float32),
        lax.psum_scatter(
            terms[3].astype(jnp.bfloat16), "group", scatter_dimension=0, tiled=True
        ).astype(jnp.float32),
        lax.psum_scatter(
            terms[4].astype(jnp.bfloat16), "group", scatter_dimension=0, tiled=True
        ).astype(jnp.float32),
    )
    totals = lax.psum((row_sums[0], row_sums[1], row_sums[2], row_sums[3], row_sums[4]), "replica")
    owned = tuple(
        (
            lax.dynamic_slice_in_dim(
                item, column * (item.shape[1] // replicas), item.shape[1] // replicas, 1
            )
            for item in totals
        )
    )
    return owned[:4] + (owned[4].reshape(-1),)


def body(
    hidden_in,
    cotangent,
    segment_ids,
    positions,
    w_qkv,
    w_out,
    w_gate_up,
    w_down,
    norm_gains,
    first_qkv,
    first_out,
    first_gate_up,
    first_down,
    first_gains,
    second_qkv,
    second_out,
    second_gate_up,
    second_down,
    second_gains,
):
    groups = lax.axis_size("group")
    replicas = lax.axis_size("replica")
    direct = (groups, replicas) == (4, 8)
    if direct:
        full_qkv, full_out, full_gate_up, full_down = gather_weights(
            groups, replicas, w_qkv, w_out, w_gate_up, w_down
        )
    else:
        full_qkv, full_out, full_gate_up, full_down = (
            lax.all_gather(w_qkv, "group", axis=0, tiled=True),
            lax.all_gather(w_out, "group", axis=0, tiled=True),
            lax.all_gather(w_gate_up, "group", axis=0, tiled=True),
            lax.all_gather(w_down, "group", axis=0, tiled=True),
        )
    block_out, grad_in, terms = layer_grads(
        hidden_in, cotangent, segment_ids, positions, full_qkv, full_out, full_gate_up, full_down, norm_gains
    )
    if direct:
        owned = sum_gradients(groups, replicas, *terms)
    else:
        owned = owned_sums(groups, replicas, terms)
    column = lax.axis_index("replica")

    def old_columns(weight):
        width = weight.shape[1] // replicas
        return lax.dynamic_slice_in_dim(weight, column * width, width, 1).astype(jnp.float32)

    moment_qkv, new_qkv = adam_step(
        owned[0], first_qkv, second_qkv, old_columns(w_qkv), weight_decay
    )
    moment_out, new_out = adam_step(
        owned[1], first_out, second_out, old_columns(w_out), weight_decay
    )
    moment_gate_up, new_gate_up = adam_step(
        owned[2], first_gate_up, second_gate_up, old_columns(w_gate_up), weight_decay
    )
    moment_down, new_down = adam_step(
        owned[3], first_down, second_down, old_columns(w_down), weight_decay
    )
    grad_gains = owned[4]
    share = grad_gains.shape[0]
    owner = lax.axis_index("group") * replicas + column
    old_gains = lax.dynamic_slice_in_dim(norm_gains, owner * share, share, 0)
    moment_gains, new_gains = adam_step(grad_gains, first_gains, second_gains, old_gains, 0.0)
    return (
        block_out,
        grad_in,
        owned[0],
        owned[1],
        owned[2],
        owned[3],
        grad_gains,
        moment_qkv,
        moment_out,
        moment_gate_up,
        moment_down,
        moment_gains,
        new_qkv,
        new_out,
        new_gate_up,
        new_down,
        new_gains,
    )


def solution(mesh):
    in_specs = (
        P(("group", "replica"), None),
        P(("group", "replica"), None),
        P(("group", "replica")),
        P(("group", "replica")),
        P("group", None),
        P("group", None),
        P("group", None),
        P("group", None),
        P(),
        P("group", "replica"),
        P("group", "replica"),
        P("group", "replica"),
        P("group", "replica"),
        P(("group", "replica")),
        P("group", "replica"),
        P("group", "replica"),
        P("group", "replica"),
        P("group", "replica"),
        P(("group", "replica")),
    )
    out_specs = (
        P(("group", "replica"), None),
        P(("group", "replica"), None),
        P("group", "replica"),
        P("group", "replica"),
        P("group", "replica"),
        P("group", "replica"),
        P(("group", "replica")),
        P("group", "replica"),
        P("group", "replica"),
        P("group", "replica"),
        P("group", "replica"),
        P(("group", "replica")),
        P("group", "replica"),
        P("group", "replica"),
        P("group", "replica"),
        P("group", "replica"),
        P(("group", "replica")),
    )
    return jax.shard_map(body, mesh=mesh, in_specs=in_specs, out_specs=out_specs, check_vma=False)
```
